32 devices in a mesh: ep: 8 (over y, x, core), tp: 4 (over z).
Axes of the slice: x: 2, y: 2, z: 4, core: 2. Of those that a mesh axis runs over, the one named last changes fastest.
Arguments:
- hidden_in: bfloat16 [4096, 2048], P(('ep', 'tp')), may hold values from -6 to 6
- w_query: bfloat16 [2048, 2048], P(('ep', 'tp')), may hold values from -0.125 to 0.125
- w_key: bfloat16 [2048, 2048], P(('ep', 'tp')), may hold values from -0.125 to 0.125
- w_value: bfloat16 [2048, 2048], P(('ep', 'tp')), may hold values from -0.125 to 0.125
- w_output: bfloat16 [2048, 2048], P(('ep', 'tp')), may hold values from -0.5 to 0.5
- w_router: bfloat16 [2048, 64], P(('ep', 'tp')), may hold values from -0.0625 to 0.0625
- gain_attn: bfloat16 [2048], P(('ep', 'tp')), may hold values from 0.25 to 1.75
- gain_ffn: bfloat16 [2048], P(('ep', 'tp')), may hold values from 0.25 to 1.75
- gain_query: bfloat16 [2048], P(('ep', 'tp')), may hold values from 0.25 to 1.75
- gain_key: bfloat16 [2048], P(('ep', 'tp')), may hold values from 0.25 to 1.75
- w_gate: bfloat16 [64, 2048, 1024], P('ep', None, 'tp'), may hold values from -0.125 to 0.125
- w_up: bfloat16 [64, 2048, 1024], P('ep', None, 'tp'), may hold values from -0.125 to 0.125
- w_down: bfloat16 [64, 1024, 2048], P('ep', 'tp'), may hold values from -6 to 6
- expert_ids: int32 [4096, 8], P(('ep', 'tp')), may hold values from 0 to 63, all different within a row; in each aligned block of 128 rows (0 to 127, 128 to 255, ...) at most 32 rows name the same one
- grad_out: bfloat16 [4096, 2048], P(('ep', 'tp')), may hold values from -6 to 6
Outputs:
- block_out: bfloat16 [4096, 2048], P(('ep', 'tp'))
- grad_input: float32 [4096, 2048], P(('ep', 'tp'))
- grad_query: float32 [2048, 2048], P(('ep', 'tp'))
- grad_key: float32 [2048, 2048], P(('ep', 'tp'))
- grad_value: float32 [2048, 2048], P(('ep', 'tp'))
- grad_output: float32 [2048, 2048], P(('ep', 'tp'))
- grad_router: float32 [2048, 64], P(('ep', 'tp'))
- grad_gain_attn: float32 [2048], P(('ep', 'tp'))
- grad_gain_ffn: float32 [2048], P(('ep', 'tp'))
- grad_gain_query: float32 [2048], P(('ep', 'tp'))
- grad_gain_key: float32 [2048], P(('ep', 'tp'))
- grad_gate: float32 [64, 2048, 1024], P('ep', None, 'tp')
- grad_up: float32 [64, 2048, 1024], P('ep', None, 'tp')
- grad_down: float32 [64, 1024, 2048], P('ep', 'tp')
The draws below stay inside these ranges and needn't reach their ends.
Inputs may be any that keep to these rules, and one draw needn't show every extreme that they name: `expert_ids`: in each aligned block of 128 rows no expert is named by more than 32 rows, a bound that some block reaches.
All inputs are finite; a program needn't handle non-finite values.
Results may differ from the reference program's by a relative error of at most 0.019.
Values may be sent and summed in bfloat16 or wider, within the bound.
No kernel may reach another device: no remote copies, remote signals or barrier semaphores. Data moves between devices by JAX's collectives and lax.ppermute only.
A program may use at most 448 MiB of HBM per device.

```python
import math
import jax
import jax.numpy as jnp
import numpy as np
from jax import lax

D = 2048
HEADS = 16
HEAD_DIM = 128
EXPERTS = 64
TOP = 8
FF_EXP = 1024
TOK_DEV = 128
CAP = 32
TOKENS = 4096


def raised(values, key, source, target, shards_of, factor):
    def block_of(dim):
        return (jnp.arange(values.shape[dim]) // (values.shape[dim] // shards_of)).reshape((-1,) + (1,) * (values.ndim - 1 - dim))

    one_side = jax.random.permutation(key, shards_of)[block_of(target)]
    far = (block_of(target) + shards_of // 2) % shards_of
    return jnp.where((block_of(source) == one_side) | (block_of(source) == far), factor * values, values)


def levels(rng, shape, shards, least, top_value):
    gain, own = 1.0, jax.random.fold_in(rng, 6)
    for dim, shards_of in shards:
        steps = jnp.exp(jax.random.uniform(jax.random.fold_in(own, dim), (shards_of,), jnp.float32, least / len(shards), top_value / len(shards)))
        gain = gain * jnp.repeat(steps, shape[dim] // shards_of).reshape([-1 if axis == dim else 1 for axis in range(len(shape))])
    return gain


def shared_out(rng, own, number, rows, count, top, limit, skew):
    order = jax.random.permutation(rng, count)
    heavy_load, common = portions_of(count, rows * top, limit, skew, True), portions_of(count, rows * top, limit, skew, False)
    places = jnp.arange(count)

    def named(lengths, turn):
        used = int((lengths > 0).sum())
        fixed = max(1, used // 4)
        passed = fixed + (places - fixed + turn * (used - fixed)) % max(1, count - fixed)
        return jnp.zeros((count,), jnp.int32).at[order[jnp.where(places < fixed, places, passed)]].set(jnp.asarray(lengths, jnp.int32))

    lengths = jnp.where(number % 4 == 0, named(heavy_load, number // 4), named(common, number - number // 4 - 1))
    mixed = jax.random.permutation(jax.random.fold_in(own, 3), count)
    source_of, taker = mixed[0:count // 2 * 2:2], mixed[1:count // 2 * 2:2]
    slack = jnp.minimum(lengths[source_of] - 1, limit - lengths[taker]) // 2
    slack = jnp.where((source_of == order[0]) | (taker == order[0]) | (lengths[taker] == 0), 0, jnp.maximum(slack, 0))
    passed = jax.random.randint(jax.random.fold_in(own, 4), (count // 2,), 0, 1 << 20) % (slack + 1)
    lengths = lengths.at[source_of].add(-passed).at[taker].add(passed)
    items = jnp.searchsorted(jnp.cumsum(lengths), jnp.arange(rows * top), side="right").astype(jnp.int32)
    listing = items.reshape(top, rows).T
    listing = listing[jax.random.permutation(jax.random.fold_in(own, 1), rows)]
    turn = jax.random.randint(jax.random.fold_in(own, 2), (rows, 1), 0, top)
    return jnp.take_along_axis(listing, (jnp.arange(top)[None, :] + turn) % top, axis=1)


def portions_of(number_of, total, limit, skew, full):
    loads = [(1 << 20) // math.isqrt(grade ** skew) + 1 for grade in range(1, number_of + 1)]
    largest = limit if full else min(limit, max(-(-total // number_of), total * loads[0] // sum(loads)))
    least = 1 if total - largest >= number_of - 1 else 0
    given, surplus = [largest] + [least] * (number_of - 1), total - largest - least * (number_of - 1)
    while surplus > 0:
        free = [i for i in range(1, number_of) if given[i] < largest] or [i for i in range(1, number_of) if given[i] < limit]
        pool, budget = sum([loads[i] for i in free]), surplus
        for i in free:
            more = min(limit - given[i], max(1, budget * loads[i] // pool), surplus)
            given[i] = given[i] + more
            surplus = surplus - more
    return np.array(given)


def gaussian(key, dims, scale, limit, pieces=(), kind=jnp.bfloat16):
    level = levels(key, dims, pieces, -0.22, 0.18) if pieces else 1.0
    entries = jax.random.normal(key, dims, jnp.float32) * scale * level
    return jnp.minimum(jnp.maximum(entries, -limit), limit).astype(kind)


def gaussian_with(own_key, shape, width, limit, split, heavy, held_as=jnp.bfloat16):
    array = width * jax.random.normal(own_key, shape, jnp.float32)
    if split:
        array = array * levels(own_key, shape, split, -0.22, 0.18)
    return jnp.clip(raised(array, jax.random.fold_in(own_key, 3), *heavy), -limit, limit).astype(held_as)


def setup_inputs(seed: int = 0) -> dict:
    splits = jax.random.split(jax.random.key(seed), 16)
    hidden_in = gaussian_with(splits[0], (TOKENS, D), 1.0, 6.0, ((0, 32),), (0, 1, 32, 2.75))
    w_query = gaussian(splits[1], (D, D), D ** -0.5, 0.125, ((0, 32),))
    w_key = gaussian(splits[2], (D, D), D ** -0.5, 0.125, ((0, 32),))
    w_value = gaussian(splits[3], (D, D), D ** -0.5, 0.125, ((0, 32),))
    w_output = gaussian(splits[4], (D, D), (D // 16) ** -0.5, 0.5, ((0, 32),))
    w_router = gaussian(splits[5], (D, EXPERTS), (4 * D) ** -0.5, 0.0625, ((0, 32),))
    gain_attn = jnp.clip(1.0 + 0.15 * jax.random.normal(splits[6], (D,), jnp.float32), 0.25, 1.75).astype(jnp.bfloat16)
    gain_ffn = jnp.clip(1.0 + 0.15 * jax.random.normal(splits[7], (D,), jnp.float32), 0.25, 1.75).astype(jnp.bfloat16)
    gain_query = jnp.clip(1.0 + 0.15 * jax.random.normal(splits[8], (D,), jnp.float32), 0.25, 1.75).astype(jnp.bfloat16)
    gain_key = jnp.clip(1.0 + 0.15 * jax.random.normal(splits[9], (D,), jnp.float32), 0.25, 1.75).astype(jnp.bfloat16)
    w_gate = gaussian(splits[10], (EXPERTS, D, FF_EXP), D ** -0.5, 0.125, ((0, 8), (2, 4)))
    w_up = gaussian(splits[11], (EXPERTS, D, FF_EXP), D ** -0.5, 0.125, ((0, 8), (2, 4)))
    w_down = gaussian(splits[12], (EXPERTS, FF_EXP, D), (EXPERTS / (TOP * FF_EXP) ** 0.5 * 1.7), 6.0, ((0, 8), (1, 4)))
    expert_ids_keys = jax.random.split(jax.random.fold_in(splits[13], 1), TOKENS // TOK_DEV)
    expert_ids_turns = jax.random.permutation(jax.random.fold_in(splits[13], 3), TOKENS // TOK_DEV)
    expert_ids = jax.vmap(lambda own, number: shared_out(jax.random.fold_in(splits[13], 2), own, number, TOK_DEV, EXPERTS, TOP, CAP, 4))(expert_ids_keys, expert_ids_turns).reshape((TOKENS, TOP))
    grad_out = gaussian(splits[14], (TOKENS, D), 1.0, 6.0, ((0, 32),))
    return dict(hidden_in=hidden_in, w_query=w_query, w_key=w_key, w_value=w_value, w_output=w_output, w_router=w_router, gain_attn=gain_attn, gain_ffn=gain_ffn, gain_query=gain_query, gain_key=gain_key, w_gate=w_gate, w_up=w_up, w_down=w_down, expert_ids=expert_ids, grad_out=grad_out)


epsilon = 1e-05
rope_base = 10000.0
masked_value = -1e+30

@jax.custom_vjp
def low(v):
    return lax.optimization_barrier(v.astype(jnp.bfloat16)).astype(jnp.float32)

@jax.custom_vjp
def low_back(v):
    return v

def low_keep(v):
    return (low(v), None)

def low_pass(kept, grad):
    return (grad,)

def back_keep(v):
    return (v, None)

def back_low(kept, grad):
    return (low(grad),)
low.defvjp(low_keep, low_pass)
low_back.defvjp(back_keep, back_low)

def matmul(left, right):
    return jnp.dot(left, right, precision=lax.Precision.HIGHEST)

def rms_norm(values, gain_vals):
    inv_scale = lax.rsqrt(lax.optimization_barrier(jnp.mean(values * values, axis=-1, keepdims=True)) + epsilon)
    return values * inv_scale * gain_vals

def rotate(values):
    half_dim = HEAD_DIM // 2
    length = values.shape[1]
    position = jnp.arange(length, dtype=jnp.int32).astype(values.dtype)
    frequency = jnp.exp(jnp.arange(half_dim, dtype=jnp.int32).astype(values.dtype) * (-2.0 * math.log(rope_base) / HEAD_DIM))
    angles = position[:, None] * frequency[None, :]
    cosines = jnp.cos(angles)[None, :, None, :]
    sines = jnp.sin(angles)[None, :, None, :]
    first_half = values[..., :half_dim]
    second = values[..., half_dim:]
    return jnp.concatenate([first_half * cosines - second * sines, second * cosines + first_half * sines], axis=-1)

def forward(hidden, w_query, w_key, w_value, w_output, w_router, gain_attn, gain_ffn, gain_query, gain_key, w_gate, w_up, w_down, expert_ids):
    blocks = TOKENS // TOK_DEV
    pair_total = TOKENS * TOP
    normed = low(rms_norm(hidden, gain_attn))
    queries = low_back(matmul(normed, w_query))
    keys_raw = low_back(matmul(normed, w_key))
    values_low = low_back(low(matmul(normed, w_value)))
    query_rot = low_back(low(rotate(rms_norm(queries, gain_query).reshape(blocks, TOK_DEV, HEADS, HEAD_DIM))))
    key_rot = low_back(low(rotate(rms_norm(keys_raw, gain_key).reshape(blocks, TOK_DEV, HEADS, HEAD_DIM))))
    scores = low_back(jnp.einsum('bqhd,bkhd->bhqk', query_rot, key_rot, precision=lax.Precision.HIGHEST) * (1.0 / math.sqrt(HEAD_DIM)))
    causal = jnp.arange(TOK_DEV, dtype=jnp.int32)[:, None] >= jnp.arange(TOK_DEV, dtype=jnp.int32)[None, :]
    scores = jnp.where(causal[None, None], scores, masked_value)
    row_peak = lax.optimization_barrier(jnp.max(scores, axis=-1, keepdims=True))
    exponent = jnp.exp(scores - row_peak)
    att_probs = exponent / lax.optimization_barrier(jnp.sum(exponent, axis=-1, keepdims=True))
    attended = jnp.einsum('bhqk,bkhd->bqhd', low(att_probs), values_low.reshape(blocks, TOK_DEV, HEADS, HEAD_DIM), precision=lax.Precision.HIGHEST)
    attended = low_back(low(attended.reshape(TOKENS, D)))
    mixed = hidden + low_back(matmul(attended, w_output))
    normed_ffn = low(rms_norm(mixed, gain_ffn))
    router_probs = jax.nn.softmax(matmul(normed_ffn, w_router), axis=-1)
    gate_values = jnp.take_along_axis(router_probs, expert_ids, axis=1).reshape(-1)
    block_ids = expert_ids.reshape(blocks, TOK_DEV * TOP)
    onehot = (block_ids[..., None] == jnp.arange(EXPERTS, dtype=jnp.int32)).astype(jnp.int32)
    slot_index = lax.optimization_barrier(jnp.sum(jnp.cumsum(onehot, axis=1) * onehot, axis=-1)) - 1
    block_index = jnp.arange(blocks, dtype=jnp.int32)[:, None]
    place_index = ((block_ids * blocks + block_index) * CAP + slot_index).reshape(-1)
    source = jnp.full((EXPERTS * blocks * CAP,), pair_total, dtype=jnp.int32)
    source = source.at[place_index].set(jnp.arange(pair_total, dtype=jnp.int32)).reshape(EXPERTS, blocks * CAP)

    def expert_rows(inputs):
        source_rows, gate_w, up_w, down_w = inputs
        filled = source_rows < pair_total
        picked = jnp.minimum(source_rows, pair_total - 1)
        token_of = picked // TOP
        rows_in = low_back(jnp.where(filled[:, None], normed_ffn[token_of], 0.0))
        gate_pre = low_back(matmul(rows_in, gate_w))
        up_pre = low_back(matmul(rows_in, up_w))
        inner_act = low(jax.nn.silu(gate_pre) * up_pre)
        result = low_back(low(matmul(inner_act, down_w)))
        weight_rows = jnp.where(filled, gate_values[picked], 0.0)
        return weight_rows[:, None] * result
    weighted = lax.map(jax.checkpoint(expert_rows), (source, w_gate, w_up, w_down))
    token_all = (jnp.minimum(source, pair_total - 1) // TOP).reshape(-1)
    expert_sum = jnp.zeros((TOKENS, D), hidden.dtype).at[token_all].add(weighted.reshape(-1, D))
    return mixed + expert_sum

def reference(hidden_in, w_query, w_key, w_value, w_output, w_router, gain_attn, gain_ffn, gain_query, gain_key, w_gate, w_up, w_down, expert_ids, grad_out):

    def closed(hidden, wq_f, wk_f, wv_f, wo_f, wr_f, ga_f, gf_f, gq_f, gk_f, wg_f, wu_f, wd_f):
        return forward(hidden, wq_f, wk_f, wv_f, wo_f, wr_f, ga_f, gf_f, gq_f, gk_f, wg_f, wu_f, wd_f, expert_ids)
    output, pullback = jax.vjp(closed, hidden_in.astype(jnp.float32), w_query.astype(jnp.float32), w_key.astype(jnp.float32), w_value.astype(jnp.float32), w_output.astype(jnp.float32), w_router.astype(jnp.float32), gain_attn.astype(jnp.float32), gain_ffn.astype(jnp.float32), gain_query.astype(jnp.float32), gain_key.astype(jnp.float32), w_gate.astype(jnp.float32), w_up.astype(jnp.float32), w_down.astype(jnp.float32))
    grad_vals = pullback(grad_out.astype(jnp.float32))
    return (output.astype(jnp.bfloat16), grad_vals[0], grad_vals[1], grad_vals[2], grad_vals[3], grad_vals[4], grad_vals[5], grad_vals[6], grad_vals[7], grad_vals[8], grad_vals[9], grad_vals[10], grad_vals[11], grad_vals[12])
```

```python
import math

import jax
import jax.numpy as jnp
from jax import lax
from jax.experimental import pallas as pl
from jax.experimental.pallas import tpu as pltpu
from jax.sharding import PartitionSpec as P

HEADS = 16
HEAD_DIM = 128
CAP = 32


epsilon = 1e-05
rope_base = 10000.0
masked_value = -1e30
low = jnp.bfloat16
wide = jnp.float32


def rope_tables(length, head_dim):
    half_dim = head_dim // 2
    position = jnp.arange(length, dtype=jnp.float32)
    frequency = jnp.exp(
        jnp.arange(half_dim, dtype=jnp.float32) * (-2.0 * math.log(rope_base) / head_dim)
    )
    angles = position[:, None] * frequency[None, :]
    return (jnp.cos(angles)[:, None, :], jnp.sin(angles)[:, None, :])


def rotate(values, cosines, sines):
    half_dim = values.shape[-1] // 2
    first_half = values[..., :half_dim]
    second = values[..., half_dim:]
    return jnp.concatenate(
        [first_half * cosines - second * sines, second * cosines + first_half * sines], axis=-1
    )


def unrotate(grad_vals, cosines, sines):
    half_dim = grad_vals.shape[-1] // 2
    first_half = grad_vals[..., :half_dim]
    second = grad_vals[..., half_dim:]
    return jnp.concatenate(
        [first_half * cosines + second * sines, second * cosines - first_half * sines], axis=-1
    )


def rms_back(grad_normed, unit_vals, gain_vals, inv_scale):
    scaled = grad_normed * gain_vals
    return inv_scale * (scaled - unit_vals * jnp.mean(scaled * unit_vals, axis=-1, keepdims=True))


def bounce(values):
    return lax.optimization_barrier(values.astype(low)).astype(wide)


class Grid:
    axes = "yxcz"

    def __init__(self):
        self.ep, self.tp = lax.axis_size("ep"), lax.axis_size("tp")
        chips = self.ep // 2
        nx = math.isqrt(chips)
        while chips % nx:
            nx -= 1
        self.size = {"y": chips // nx, "x": nx, "c": 2, "z": self.tp}
        self.stride = {"y": 2 * nx, "x": 2, "c": 1}
        self.shape = tuple(self.size[axis] for axis in self.axes)

    def place(self, axis):
        if axis == "z":
            return lax.axis_index("tp")
        return lax.axis_index("ep") // self.stride[axis] % self.size[axis]

    def shift(self, values, axis, step):
        count = self.size[axis]
        if axis == "z":
            return lax.ppermute(values, "tp", [(i, (i + step) % count) for i in range(count)])
        stride = self.stride[axis]
        pairs = []
        for i in range(self.ep):
            own = i // stride % count
            pairs.append((i, i + ((own + step) % count - own) * stride))
        return lax.ppermute(values, "ep", pairs)

    def gather(self, values, order):
        values = values[None, None, None, None]
        for axis in order:
            dim, count, own = self.axes.index(axis), self.size[axis], self.place(axis)
            parts = [values] + [self.shift(values, axis, step) for step in range(1, count)]
            shape = list(values.shape)
            shape[dim] = count
            values = jnp.zeros(shape, values.dtype)
            for step, part in enumerate(parts):
                values = lax.dynamic_update_slice_in_dim(
                    values, part, (own - step) % count, dim
                )
        return values

    def gather_rows(self, values, orders):
        share = values.shape[0] // len(orders)
        parts = [
            self.gather(values[i * share : (i + 1) * share], order)
            for i, order in enumerate(orders)
        ]
        return jnp.concatenate(parts, axis=4).reshape((-1,) + values.shape[1:])

    def reduce_scatter(self, values, order):
        left = list(self.axes)
        kind = values.dtype
        values = values.reshape(self.shape + values.shape[1:])
        for axis in order:
            dim, count, own = left.index(axis), self.size[axis], self.place(axis)

            def part(step):
                return lax.dynamic_index_in_dim(
                    values, (own - step) % count, dim, keepdims=False
                )

            total = part(0).astype(wide)
            for step in range(1, count):
                total = total + self.shift(part(step), axis, -step).astype(wide)
            values = total.astype(kind)
            left.remove(axis)
        return values


gather_orders = ("zxyc", "zyxc", "xzyc", "yzxc")
reduce_orders = ("cyxz", "cxyz", "cyzx", "cxzy")
nt_dims = (((1,), (1,)), ((), ()))
tn_dims = (((0,), (0,)), ((), ()))


def one_hot(slots):
    experts, tokens = slots.shape
    place = lax.broadcasted_iota(jnp.int32, (experts, CAP, tokens), 1).astype(wide) + 1.0
    return (slots[:, None, :] == place).astype(wide).reshape(experts * CAP, tokens)


def dot(left, right, dims=(((1,), (0,)), ((), ()))):
    return lax.dot_general(left, right, dims, preferred_element_type=wide)


def spread(target, rows, block):
    for e in range(target.shape[0]):
        target[e, block * CAP : (block + 1) * CAP, :] = rows[e * CAP : (e + 1) * CAP]


def joined_rows(source, block):
    return jnp.concatenate(
        [source[e, block * CAP : (block + 1) * CAP, :] for e in range(source.shape[0])], axis=0
    )


def weight_copies(sources, targets, sems):
    return [
        [
            pltpu.make_async_copy(source.at[e], target.at[e], sems.at[i, e])
            for i, (source, target) in enumerate(zip(sources, targets, strict=True))
        ]
        for e in range(targets[0].shape[0])
    ]


def forward_kernel(
    slots_ref,
    router_ref,
    x_ref,
    gate_hbm,
    up_hbm,
    down_hbm,
    y0_ref,
    y1_ref,
    y2_ref,
    y3_ref,
    gates_ref,
    pre_ref,
    inner_ref,
    rows_hbm,
    gate_w,
    up_w,
    down_w,
    rows_v,
    out_v,
    gate_rows,
    w_sems,
    row_sem,
):
    step = pl.program_id(0)
    chunk = x_ref.shape[0]
    experts, depth, _ = rows_v.shape
    hidden = gate_w.shape[2]
    copies = weight_copies((gate_hbm, up_hbm, down_hbm), (gate_w, up_w, down_w), w_sems)

    def rows_copy(at):
        return pltpu.make_async_copy(
            rows_v, rows_hbm.at[:, pl.ds(at * depth, depth), :], row_sem.at[0]
        )

    @pl.when(step == 0)
    def _():
        for expert in copies:
            for copy in expert:
                copy.start()

    @pl.when(step > 0)
    def _():
        rows_copy(step - 1).wait()

    picks = []
    for b in range(chunk):
        tokens = x_ref[b]
        logits = dot(router_ref[...], tokens, nt_dims)
        exponent = jnp.exp(logits - jnp.max(logits, axis=0, keepdims=True))
        probs = exponent / jnp.sum(exponent, axis=0, keepdims=True)
        gates = probs[:experts]
        gates_ref[b] = gates
        pick = one_hot(slots_ref[b])
        spread_gates = jnp.broadcast_to(gates[:, None, :], (experts, CAP, gates.shape[1]))
        gated = jnp.sum(pick * spread_gates.reshape(pick.shape), axis=1, keepdims=True)
        spread(gate_rows, gated, b)
        pick = pick.astype(low)
        spread(rows_v, dot(pick, tokens).astype(low), b)
        picks.append(pick)
    rows_copy(step).start()

    for e in range(experts):

        @pl.when(step == 0)
        def _(e=e):
            for copy in copies[e]:
                copy.wait()

        rows = rows_v[e]
        gate_pre = dot(rows, gate_w[e])
        up_pre = dot(rows, up_w[e])
        pre_ref[e, :, :hidden] = gate_pre
        pre_ref[e, :, hidden:] = up_pre
        inner = (gate_pre * jax.nn.sigmoid(gate_pre) * up_pre).astype(low).astype(wide)
        scaled = (inner * gate_rows[e]).astype(low)
        inner_ref[e] = scaled
        out_v[e] = dot(scaled, down_w[e]).astype(low)

    for b in range(chunk):
        total = dot(picks[b], joined_rows(out_v, b), tn_dims).astype(low)
        share = total.shape[0] // 4
        for i, y_ref in enumerate((y0_ref, y1_ref, y2_ref, y3_ref)):
            y_ref[b] = total[i * share : (i + 1) * share]

    @pl.when(step == pl.num_programs(0) - 1)
    def _():
        rows_copy(step).wait()


def backward_kernel(
    slots_ref,
    gates_ref,
    g_ref,
    pre_ref,
    gate_hbm,
    up_hbm,
    down_hbm,
    x0_ref,
    x1_ref,
    x2_ref,
    x3_ref,
    grads_ref,
    dgate_ref,
    dup_ref,
    rows_hbm,
    gate_w,
    up_w,
    down_w,
    rows_v,
    out_v,
    gate_rows,
    grad_rows,
    w_sems,
    row_sem,
):
    step = pl.program_id(0)
    chunk = g_ref.shape[0]
    experts, depth, _ = rows_v.shape
    hidden = gate_w.shape[2]
    copies = weight_copies((gate_hbm, up_hbm, down_hbm), (gate_w, up_w, down_w), w_sems)

    def rows_copy(at):
        return pltpu.make_async_copy(
            rows_v, rows_hbm.at[:, pl.ds(at * depth, depth), :], row_sem.at[0]
        )

    @pl.when(step == 0)
    def _():
        for expert in copies:
            for copy in expert:
                copy.start()

    @pl.when(step > 0)
    def _():
        rows_copy(step - 1).wait()

    picks = []
    for b in range(chunk):
        gates = gates_ref[b]
        pick = one_hot(slots_ref[b])
        spread_gates = jnp.broadcast_to(gates[:, None, :], (experts, CAP, gates.shape[1]))
        gated = jnp.sum(pick * spread_gates.reshape(pick.shape), axis=1, keepdims=True)
        spread(gate_rows, gated, b)
        pick = pick.astype(low)
        spread(rows_v, dot(pick, g_ref[b]).astype(low), b)
        picks.append(pick)
    rows_copy(step).start()

    for e in range(experts):

        @pl.when(step == 0)
        def _(e=e):
            for copy in copies[e]:
                copy.wait()

        pulled = dot(rows_v[e], down_w[e], nt_dims)
        gate_pre = pre_ref[e, :, :hidden]
        up_pre = pre_ref[e, :, hidden:]
        sigmoid = jax.nn.sigmoid(gate_pre)
        silu = gate_pre * sigmoid
        inner = (silu * up_pre).astype(low).astype(wide)
        grad_rows[e] = jnp.sum(inner * pulled, axis=1, keepdims=True)
        grad_inner = pulled * gate_rows[e]
        dgate = (grad_inner * up_pre * sigmoid * (1.0 + gate_pre * (1.0 - sigmoid))).astype(low)
        dup = (grad_inner * silu).astype(low)
        dgate_ref[e] = dgate
        dup_ref[e] = dup
        out_v[e] = (dot(dgate, gate_w[e], nt_dims) + dot(dup, up_w[e], nt_dims)).astype(low)

    for b in range(chunk):
        total = dot(picks[b], joined_rows(out_v, b), tn_dims).astype(low)
        share = total.shape[0] // 4
        for i, x_ref in enumerate((x0_ref, x1_ref, x2_ref, x3_ref)):
            x_ref[b] = total[i * share : (i + 1) * share]
        per_row = picks[b].astype(wide) * joined_rows(grad_rows, b)
        grads_ref[b] = jnp.sum(per_row.reshape(experts, CAP, per_row.shape[1]), axis=1)

    @pl.when(step == pl.num_programs(0) - 1)
    def _():
        rows_copy(step).wait()


def expert_calls(blocks, tokens, width, experts, hidden, chunk=4):
    depth = chunk * CAP
    rows = blocks * CAP
    quarter = tokens // 4
    any_spec = pl.BlockSpec(memory_space=pl.ANY)

    def by_block(*shape):
        return pl.BlockSpec((chunk,) + shape, lambda i: (i,) + (0,) * len(shape))

    def by_row(last):
        return pl.BlockSpec((experts, depth, last), lambda i: (0, i, 0))

    def shaped(kind, *shape):
        return jax.ShapeDtypeStruct(shape, kind)

    weights = [
        pltpu.VMEM((experts, width, hidden), low),
        pltpu.VMEM((experts, width, hidden), low),
        pltpu.VMEM((experts, hidden, width), low),
    ]
    buffers = [
        pltpu.VMEM((experts, depth, width), low),
        pltpu.VMEM((experts, depth, width), low),
        pltpu.VMEM((experts, depth, 1), wide),
    ]
    sems = [pltpu.SemaphoreType.DMA((3, experts)), pltpu.SemaphoreType.DMA((1,))]
    params = pltpu.CompilerParams(
        dimension_semantics=("arbitrary",), vmem_limit_bytes=60 * 1024 * 1024
    )
    quarters = [shaped(low, blocks, quarter, width)] * 4
    quarter_specs = [by_block(quarter, width)] * 4
    flops = 2 * experts * rows * width * (3 * hidden + 2 * tokens)
    cost = pl.CostEstimate(
        flops=flops, bytes_accessed=experts * rows * width * 6, transcendentals=0
    )
    router_rows = 64

    forward = pl.pallas_call(
        forward_kernel,
        grid=(blocks // chunk,),
        in_specs=[
            by_block(experts, tokens),
            pl.BlockSpec((router_rows, width), lambda i: (0, 0)),
            by_block(tokens, width),
            any_spec,
            any_spec,
            any_spec,
        ],
        out_specs=quarter_specs
        + [by_block(experts, tokens), by_row(2 * hidden), by_row(hidden), any_spec],
        out_shape=quarters
        + [
            shaped(wide, blocks, experts, tokens),
            shaped(wide, experts, rows, 2 * hidden),
            shaped(low, experts, rows, hidden),
            shaped(low, experts, rows, width),
        ],
        scratch_shapes=weights + buffers + sems,
        compiler_params=params,
        cost_estimate=cost,
        name="experts_forward",
    )
    backward = pl.pallas_call(
        backward_kernel,
        grid=(blocks // chunk,),
        in_specs=[
            by_block(experts, tokens),
            by_block(experts, tokens),
            by_block(tokens, width),
            by_row(2 * hidden),
            any_spec,
            any_spec,
            any_spec,
        ],
        out_specs=quarter_specs
        + [by_block(experts, tokens), by_row(hidden), by_row(hidden), any_spec],
        out_shape=quarters
        + [
            shaped(wide, blocks, experts, tokens),
            shaped(low, experts, rows, hidden),
            shaped(low, experts, rows, hidden),
            shaped(low, experts, rows, width),
        ],
        scratch_shapes=weights + buffers + [pltpu.VMEM((experts, depth, 1), wide)] + sems,
        compiler_params=params,
        cost_estimate=cost,
        name="experts_backward",
    )
    return forward, backward


def on_device(
    hidden_in,
    w_query,
    w_key,
    w_value,
    w_output,
    w_router,
    gain_attn,
    gain_ffn,
    gain_query,
    gain_key,
    w_gate,
    w_up,
    w_down,
    expert_ids,
    grad_out,
):
    tokens_dev, model_width = hidden_in.shape
    local_experts, _, hidden_units = w_gate.shape
    expert_count = w_router.shape[1]
    grid = Grid()
    blocks = grid.ep * grid.tp
    weight_rows = model_width // blocks
    both = ("ep", "tp")
    inv_root = 1.0 / math.sqrt(HEAD_DIM)

    def gathered(values):
        return lax.all_gather(values, both, axis=0, tiled=True)

    named = jnp.any(
        expert_ids[None, :, :] == jnp.arange(expert_count, dtype=jnp.int32)[:, None, None], axis=2
    )
    before = (jnp.arange(tokens_dev)[:, None] <= jnp.arange(tokens_dev)[None, :]).astype(low)
    counted = jnp.dot(named.astype(low), before, preferred_element_type=wide)
    slots = jnp.where(named, counted, 0.0).astype(low)

    shared = jnp.concatenate(
        [
            w_router,
            jnp.stack([gain_attn, gain_ffn, gain_query, gain_key], axis=1),
            jnp.zeros((w_router.shape[0], tokens_dev - expert_count - 4), low),
        ],
        axis=1,
    )
    small_all = grid.gather(jnp.concatenate([shared, slots], axis=0), "xyzc")
    small_all = small_all.reshape(blocks, weight_rows + expert_count, tokens_dev)
    shared_full = small_all[:, :weight_rows].reshape(model_width, tokens_dev)
    slots_all = small_all[:, weight_rows:]
    router_full = shared_full[:, :expert_count]
    gains = shared_full[:, expert_count : expert_count + 4].astype(wide).T
    attn_gain, ffn_gain, query_gain, key_gain = gains[0], gains[1], gains[2], gains[3]
    query_full = gathered(w_query)
    key_full = gathered(w_key)
    value_full = grid.gather_rows(w_value, gather_orders)
    output_full = grid.gather_rows(w_output, gather_orders)
    upstream_all = gathered(grad_out[None])

    inputs_full = hidden_in.astype(wide)
    scale_attn = lax.rsqrt(jnp.mean(inputs_full * inputs_full, axis=-1, keepdims=True) + epsilon)
    unit_attn = inputs_full * scale_attn
    normed_attn = (unit_attn * attn_gain).astype(low)
    query_raw = jnp.dot(normed_attn, query_full, preferred_element_type=wide)
    key_raw = jnp.dot(normed_attn, key_full, preferred_element_type=wide)
    value_raw = jnp.dot(normed_attn, value_full, preferred_element_type=wide)
    scale_query = lax.rsqrt(jnp.mean(query_raw * query_raw, axis=-1, keepdims=True) + epsilon)
    unit_query = query_raw * scale_query
    scale_key = lax.rsqrt(jnp.mean(key_raw * key_raw, axis=-1, keepdims=True) + epsilon)
    unit_key = key_raw * scale_key
    cosines, sines = rope_tables(tokens_dev, HEAD_DIM)
    query_rot = rotate(
        (unit_query * query_gain).reshape(tokens_dev, HEADS, HEAD_DIM), cosines, sines
    ).astype(low)
    key_rot = rotate(
        (unit_key * key_gain).reshape(tokens_dev, HEADS, HEAD_DIM), cosines, sines
    ).astype(low)
    value_heads = value_raw.astype(low).reshape(tokens_dev, HEADS, HEAD_DIM)
    causal = jnp.arange(tokens_dev)[:, None] >= jnp.arange(tokens_dev)[None, :]
    scores = (
        jnp.einsum("qhd,khd->hqk", query_rot, key_rot, preferred_element_type=wide) * inv_root
    )
    scores = jnp.where(causal[None], scores, masked_value)
    exponent = jnp.exp(scores - jnp.max(scores, axis=-1, keepdims=True))
    att_probs = exponent / jnp.sum(exponent, axis=-1, keepdims=True)
    probs_low = att_probs.astype(low)
    attended = (
        jnp.einsum("hqk,khd->qhd", probs_low, value_heads, preferred_element_type=wide)
        .reshape(tokens_dev, model_width)
        .astype(low)
    )
    mixed = inputs_full + jnp.dot(attended, output_full, preferred_element_type=wide)
    scale_ffn = lax.rsqrt(jnp.mean(mixed * mixed, axis=-1, keepdims=True) + epsilon)
    unit_ffn = mixed * scale_ffn
    normed_ffn = (unit_ffn * ffn_gain).astype(low)
    normed_all = gathered(normed_ffn[None])
    router_probs = jax.nn.softmax(
        jnp.dot(normed_ffn, router_full, preferred_element_type=wide), axis=-1
    )

    first_expert = lax.axis_index("ep") * local_experts
    slots_here = lax.dynamic_slice_in_dim(slots_all, first_expert, local_experts, 1).astype(wide)
    router_turned = lax.dynamic_slice_in_dim(
        jnp.concatenate([router_full, router_full], axis=1), first_expert, expert_count, 1
    ).T
    forward, backward = expert_calls(
        blocks, tokens_dev, model_width, local_experts, hidden_units
    )
    *expert_parts, gates_all, pre_all, inner_scaled, rows_in = forward(
        slots_here, router_turned, normed_all, w_gate, w_up, w_down
    )
    expert_sum = jnp.concatenate(
        [
            grid.reduce_scatter(part, order)
            for part, order in zip(expert_parts, reduce_orders, strict=True)
        ],
        axis=0,
    )
    block_out = (mixed + expert_sum.astype(wide)).astype(low)

    *back_parts, gate_grads, grad_gate_part, grad_up_part, rows_up = backward(
        slots_here, gates_all, upstream_all, pre_all, w_gate, w_up, w_down
    )
    back_sum = jnp.concatenate(
        [
            grid.reduce_scatter(part, order)
            for part, order in zip(back_parts, reduce_orders, strict=True)
        ],
        axis=0,
    )
    gate_grads = lax.dynamic_update_slice_in_dim(
        jnp.zeros((blocks, expert_count, tokens_dev), wide), gate_grads, first_expert, 1
    )
    grad_probs = grid.reduce_scatter(gate_grads, "cyxz").T
    acc_down = jnp.einsum("erh,erd->ehd", inner_scaled, rows_up, preferred_element_type=wide)
    acc_gate = jnp.einsum("erd,erh->edh", rows_in, grad_gate_part, preferred_element_type=wide)
    acc_up = jnp.einsum("erd,erh->edh", rows_in, grad_up_part, preferred_element_type=wide)

    upstream = grad_out.astype(wide)
    grad_logits = router_probs * (
        grad_probs - jnp.sum(router_probs * grad_probs, axis=-1, keepdims=True)
    )
    grad_ffn_normed = back_sum.astype(wide) + jnp.dot(
        grad_logits, router_full.astype(wide).T, precision=lax.Precision.HIGHEST
    )
    grad_router_local = jnp.dot(
        normed_ffn.astype(wide).T, grad_logits, precision=lax.Precision.HIGHEST
    )
    grad_ffn_gain = jnp.sum(grad_ffn_normed * unit_ffn, axis=0)
    grad_mixed = upstream + rms_back(grad_ffn_normed, unit_ffn, ffn_gain, scale_ffn)
    grad_branch = grad_mixed.astype(low)

    def outer_sum(left, right, order):
        local = jnp.einsum("tc,te->ce", left, right, preferred_element_type=wide).astype(low)
        return grid.reduce_scatter(
            local.reshape(blocks, weight_rows, model_width), order
        ).astype(wide)

    grad_output = outer_sum(attended, grad_branch, "cyxz")
    grad_router = grid.reduce_scatter(
        grad_router_local.reshape(blocks, weight_rows, expert_count), "cxyz"
    )
    grad_attended = jnp.einsum(
        "te,de->td", grad_branch, output_full, preferred_element_type=wide
    ).astype(low)
    grad_heads = grad_attended.reshape(tokens_dev, HEADS, HEAD_DIM)
    grad_value_rows = (
        jnp.einsum("hqk,qhd->khd", probs_low, grad_heads, preferred_element_type=wide)
        .reshape(tokens_dev, model_width)
        .astype(low)
    )
    grad_value = outer_sum(normed_attn, grad_value_rows, "cxyz")
    grad_probs_att = jnp.einsum(
        "qhd,khd->hqk", grad_heads, value_heads, preferred_element_type=wide
    )
    grad_scores = (
        att_probs * (grad_probs_att - jnp.sum(att_probs * grad_probs_att, axis=-1, keepdims=True))
    ).astype(low)
    grad_qrot = (
        jnp.einsum("hqk,khd->qhd", grad_scores, key_rot, preferred_element_type=wide) * inv_root
    )
    grad_krot = (
        jnp.einsum("hqk,qhd->khd", grad_scores, query_rot, preferred_element_type=wide) * inv_root
    )
    grad_qnorm = unrotate(bounce(grad_qrot), cosines, sines).reshape(tokens_dev, model_width)
    grad_knorm = unrotate(bounce(grad_krot), cosines, sines).reshape(tokens_dev, model_width)
    grad_query_gain = jnp.sum(grad_qnorm * unit_query, axis=0)
    grad_key_gain = jnp.sum(grad_knorm * unit_key, axis=0)
    grad_query_raw = rms_back(grad_qnorm, unit_query, query_gain, scale_query).astype(low)
    grad_key_raw = rms_back(grad_knorm, unit_key, key_gain, scale_key).astype(low)
    grad_query = outer_sum(normed_attn, grad_query_raw, "cyxz")
    grad_key = outer_sum(normed_attn, grad_key_raw, "cxyz")
    grad_attn_normed = (
        jnp.einsum("te,ce->tc", grad_query_raw, query_full, preferred_element_type=wide)
        + jnp.einsum("te,ce->tc", grad_key_raw, key_full, preferred_element_type=wide)
        + jnp.einsum("te,ce->tc", grad_value_rows, value_full, preferred_element_type=wide)
    )
    grad_attn_gain = jnp.sum(grad_attn_normed * unit_attn, axis=0)
    grad_input = grad_mixed + rms_back(grad_attn_normed, unit_attn, attn_gain, scale_attn)
    gain_sums = jnp.stack([grad_attn_gain, grad_ffn_gain, grad_query_gain, grad_key_gain])
    gain_sums = grid.reduce_scatter(
        gain_sums.reshape(4, blocks, weight_rows).transpose(1, 0, 2), "cyxz"
    )
    return (
        block_out,
        grad_input,
        grad_query,
        grad_key,
        grad_value,
        grad_output,
        grad_router,
        gain_sums[0],
        gain_sums[1],
        gain_sums[2],
        gain_sums[3],
        acc_gate,
        acc_up,
        acc_down,
    )


def solution(mesh):
    placed = (
        P(("ep", "tp"), None),
        P(("ep", "tp"), None),
        P(("ep", "tp"), None),
        P(("ep", "tp"), None),
        P(("ep", "tp"), None),
        P(("ep", "tp"), None),
        P(("ep", "tp")),
        P(("ep", "tp")),
        P(("ep", "tp")),
        P(("ep", "tp")),
        P("ep", None, "tp"),
        P("ep", None, "tp"),
        P("ep", "tp", None),
        P(("ep", "tp"), None),
        P(("ep", "tp"), None),
    )
    return jax.shard_map(
        on_device,
        mesh=mesh,
        in_specs=placed,
        out_specs=(
            P(("ep", "tp"), None),
            P(("ep", "tp"), None),
            P(("ep", "tp"), None),
            P(("ep", "tp"), None),
            P(("ep", "tp"), None),
            P(("ep", "tp"), None),
            P(("ep", "tp"), None),
            P(("ep", "tp")),
            P(("ep", "tp")),
            P(("ep", "tp")),
            P(("ep", "tp")),
            P("ep", None, "tp"),
            P("ep", None, "tp"),
            P("ep", "tp", None),
        ),
        check_vma=False,
    )
```

```python
import functools
import math

import jax
import jax.numpy as jnp
from jax import lax
from jax.experimental import pallas as pl
from jax.experimental.pallas import tpu as pltpu
from jax.sharding import PartitionSpec as P

HEADS = 16
HEAD_DIM = 128
CAP = 32


epsilon = 1e-05
rope_base = 10000.0
masked_value = -1e30
low = jnp.bfloat16
wide = jnp.float32


def rope_tables(length, head_dim):
    half_dim = head_dim // 2
    position = jnp.arange(length, dtype=jnp.float32)
    frequency = jnp.exp(
        jnp.arange(half_dim, dtype=jnp.float32) * (-2.0 * math.log(rope_base) / head_dim)
    )
    angles = position[:, None] * frequency[None, :]
    return (jnp.cos(angles)[:, None, :], jnp.sin(angles)[:, None, :])


def rotate(values, cosines, sines):
    half_dim = values.shape[-1] // 2
    first_half = values[..., :half_dim]
    second = values[..., half_dim:]
    return jnp.concatenate(
        [first_half * cosines - second * sines, second * cosines + first_half * sines], axis=-1
    )


def unrotate(grad_vals, cosines, sines):
    half_dim = grad_vals.shape[-1] // 2
    first_half = grad_vals[..., :half_dim]
    second = grad_vals[..., half_dim:]
    return jnp.concatenate(
        [first_half * cosines + second * sines, second * cosines - first_half * sines], axis=-1
    )


def rms_back(grad_normed, unit_vals, gain_vals, inv_scale):
    scaled = grad_normed * gain_vals
    return inv_scale * (scaled - unit_vals * jnp.mean(scaled * unit_vals, axis=-1, keepdims=True))


def bounce(values):
    return lax.optimization_barrier(values.astype(low)).astype(wide)


def after(values, *needs):
    return lax.optimization_barrier((values, needs))[0]


def together(*values):
    return lax.optimization_barrier(values)


class Grid:
    axes = "yxcuw"

    def __init__(self):
        self.ep, self.tp = lax.axis_size("ep"), lax.axis_size("tp")
        chips = self.ep // 2
        nx = math.isqrt(chips)
        while chips % nx:
            nx -= 1
        nw = 2 - self.tp % 2
        self.size = {"y": chips // nx, "x": nx, "c": 2, "u": self.tp // nw, "w": nw}
        self.stride = {"y": 2 * nx, "x": 2, "c": 1, "u": nw, "w": 1}
        self.shape = tuple(self.size[axis] for axis in self.axes)

    def place(self, axis):
        whole = lax.axis_index("tp" if axis in "uw" else "ep")
        return whole // self.stride[axis] % self.size[axis]

    def shift(self, values, axis, step):
        count, stride = self.size[axis], self.stride[axis]
        pairs = []
        for i in range(self.tp if axis in "uw" else self.ep):
            own = i // stride % count
            pairs.append((i, i + ((own + step) % count - own) * stride))
        return lax.ppermute(values, "tp" if axis in "uw" else "ep", pairs)

    def gather_axis(self, values, axis):
        dim, count, own = self.axes.index(axis), self.size[axis], self.place(axis)
        parts = [values] + [self.shift(values, axis, step) for step in range(1, count)]
        shape = list(values.shape)
        shape[dim] = count
        values = jnp.zeros(shape, values.dtype)
        for step, part in enumerate(parts):
            values = lax.dynamic_update_slice_in_dim(values, part, (own - step) % count, dim)
        return values

    def gather(self, values, order):
        values = values[(None,) * len(self.axes)]
        for axis in order:
            values = self.gather_axis(values, axis)
        return values

    def gather_rows(self, values):
        rows, columns = values.shape
        values = self.gather(values, "uw")
        halves = values[..., : rows // 2, :], values[..., rows // 2 :, :]
        halves = [
            self.gather_axis(self.gather_axis(half, first), second)
            for half, (first, second) in zip(halves, ("xy", "yx"), strict=True)
        ]
        values = self.gather_axis(jnp.concatenate(halves, axis=-2), "c")
        return values.reshape(-1, columns)

    def reduce_axis(self, values, axis, axes):
        dim, count, own = axes.index(axis), self.size[axis], self.place(axis)
        values = values if isinstance(values, (list, tuple)) else [values]
        kind = values[0].dtype

        def part(step):
            return sum(
                lax.dynamic_index_in_dim(v, (own - step) % count, dim, keepdims=False).astype(wide)
                for v in values
            )

        total = part(0)
        for step in range(1, count):
            total = total + self.shift(part(step).astype(kind), axis, -step).astype(wide)
        return total.astype(kind)

    def reduce_scatter(self, values, order, axes=axes):
        for axis in order:
            values = self.reduce_axis(values, axis, axes)
            axes = axes.replace(axis, "")
        return values

    def from_line(self, values, axis):
        return [values] + [
            self.shift(values, axis, step) for step in range(1, self.size[axis])
        ]

    def columns_from_line(self, values, axis):
        rows, count, own = values.shape[0], self.size[axis], self.place(axis)
        values = values.reshape(rows, count, -1)

        def part(step):
            return lax.dynamic_index_in_dim(values, (own + step) % count, 1, keepdims=False)

        taken = jnp.stack(
            [part(0)] + [self.shift(part(step), axis, step) for step in range(1, count)]
        )
        taken = jnp.stack([taken, self.shift(taken, "c", 1)], axis=1)
        return taken.reshape(-1, taken.shape[-1])

    def rows_from_line(self, values, axis):
        count, own = self.size[axis], self.place(axis)

        def part(step):
            return lax.dynamic_index_in_dim(values, (own + step) % count, 0)

        whole = jnp.zeros(values.shape, values.dtype)
        for step in range(count):
            got = part(0) if step == 0 else self.shift(part(step), axis, step)
            whole = lax.dynamic_update_slice_in_dim(whole, got, (own - step) % count, 0)
        return whole.transpose(1, 0, 2).reshape(values.shape[1], -1)

    def reduce_first(self, pair):
        return [self.reduce_axis(v, axis, "yxuw") for v, axis in zip(pair, "yx", strict=True)]

    def reduce_both(self, pair, axis):
        left = "uw" if axis == "w" else "u"
        return [self.reduce_axis(v, axis, line + left) for v, line in zip(pair, "xy", strict=True)]

    def rows_of_both(self, pair):
        return [self.rows_from_line(v, line) for v, line in zip(pair, "xy", strict=True)]

    def reduce_second(self, pair, join):
        pair = [
            self.reduce_axis(v, axis, axis + "uw") for v, axis in zip(pair, "xy", strict=True)
        ]
        return jnp.concatenate(pair, axis=join + 2)

    def chips(self):
        return tuple(self.size[axis] for axis in "yxuw")


nt_dims = (((1,), (1,)), ((), ()))
tn_dims = (((0,), (0,)), ((), ()))


def one_hot(slots):
    experts, tokens = slots.shape
    place = lax.broadcasted_iota(jnp.int32, (experts, CAP, tokens), 1).astype(wide) + 1.0
    return (slots[:, None, :] == place).astype(wide).reshape(experts * CAP, tokens)


def dot(left, right, dims=(((1,), (0,)), ((), ()))):
    return lax.dot_general(left, right, dims, preferred_element_type=wide)


def gate_column(pick, gates):
    spread = jnp.broadcast_to(gates[:, None, :], (gates.shape[0], CAP, gates.shape[1]))
    return jnp.sum(pick * spread.reshape(pick.shape), axis=1, keepdims=True)


class Streams:
    def __init__(self, sources, targets, sems, rows_v, rows_hbm, row_sem, base):
        self.step, chunk = pl.program_id(0), rows_v.shape[0]
        experts = sources[0].shape[0]
        self.groups = [range(experts // 2), range(experts // 2, experts)]
        self.weights = [
            [
                pltpu.make_async_copy(source.at[e], target(e), sems.at[i, e])
                for i, (source, target) in enumerate(zip(sources, targets, strict=True))
                for e in group
            ]
            for group in self.groups
        ]
        block = base + self.step * chunk
        self.rows = [
            pltpu.make_async_copy(
                rows_v.at[:, e * CAP : (e + 1) * CAP, :],
                rows_hbm.at[e, pl.ds(block, chunk)],
                row_sem.at[e],
            )
            for e in range(experts)
        ]

        @pl.when(self.step == 0)
        def _():
            for copies in self.weights:
                for copy in copies:
                    copy.start()

        @pl.when(self.step > 0)
        def _():
            self.wait_rows()

    def wait_rows(self):
        for copy in self.rows:
            copy.wait()

    def send_rows(self):
        for copy in self.rows:
            copy.start()

    def wait_weights(self, group):
        @pl.when(self.step == 0)
        def _():
            for copy in self.weights[group]:
                copy.wait()

    def end(self):
        @pl.when(self.step == pl.num_programs(0) - 1)
        def _():
            self.wait_rows()


def write_parts(targets, block, total):
    share = total.shape[0] // len(targets)
    for i, target in enumerate(targets):
        target[block] = total[i * share : (i + 1) * share]


def forward_kernel(base, kept, parts, _, slots_ref, router_ref, x_ref, *refs):
    weights, refs = refs[:3], refs[3:]
    refs = refs[kept:]
    y_refs, refs = refs[:parts], refs[parts:]
    gates_ref, pre_ref, inner_ref, rows_hbm = refs[:4]
    joint_w, down_w, rows_v, out_v, gate_rows, w_sems, row_sems = refs[4:]
    chunk, _, width = x_ref.shape
    experts, hidden, _ = down_w.shape
    depth = chunk * CAP
    targets = (
        lambda e: joint_w.at[e, :, :hidden],
        lambda e: joint_w.at[e, :, hidden:],
        lambda e: down_w.at[e],
    )
    streams = Streams(weights, targets, w_sems, rows_v, rows_hbm, row_sems, base)
    picks = []
    for b in range(chunk):
        tokens = x_ref[b]
        logits = dot(tokens, router_ref[...]).T
        exponent = jnp.exp(logits - jnp.max(logits, axis=0, keepdims=True))
        gates = (exponent / jnp.sum(exponent, axis=0, keepdims=True))[:experts]
        gates_ref[b] = gates
        pick = one_hot(slots_ref[b])
        gate_rows[b] = gate_column(pick, gates)
        picks.append(pick.astype(low))
        rows_v[b] = dot(picks[b], tokens).astype(low)
    streams.send_rows()
    for e in range(experts):
        at = slice(e * CAP, (e + 1) * CAP)
        for i, group in enumerate(streams.groups):
            if e == group.start:
                streams.wait_weights(i)
        pre = dot(rows_v[:, at, :].reshape(depth, width), joint_w[e])
        pre_ref[e] = pre
        gate_pre, up_pre = pre[:, :hidden], pre[:, hidden:]
        inner = (gate_pre * jax.nn.sigmoid(gate_pre) * up_pre).astype(low).astype(wide)
        scaled = (inner * gate_rows[:, at, :].reshape(depth, 1)).astype(low)
        inner_ref[e] = scaled
        out = dot(scaled, down_w[e]).astype(low)
        out_v[:, at, :] = out.reshape(chunk, CAP, width)
    for b in range(chunk):
        write_parts(y_refs, b, dot(picks[b], out_v[b], tn_dims).astype(low))
    streams.end()


def backward_kernel(base, kept, parts, _, slots_ref, gates_ref, g_ref, pre_ref, *refs):
    weights, refs = refs[:3], refs[3:]
    refs = refs[kept:]
    x_refs, refs = refs[:parts], refs[parts:]
    grads_ref, dgate_ref, dup_ref, rows_hbm = refs[:4]
    joint_w, down_w, rows_v, out_v, gate_rows, grad_rows, w_sems, row_sems = refs[4:]
    chunk, tokens, width = g_ref.shape
    experts, _, hidden = down_w.shape
    depth = chunk * CAP
    targets = (
        lambda e: joint_w.at[e, :hidden],
        lambda e: joint_w.at[e, hidden:],
        lambda e: down_w.at[e],
    )
    streams = Streams(weights, targets, w_sems, rows_v, rows_hbm, row_sems, base)
    picks = []
    for b in range(chunk):
        pick = one_hot(slots_ref[b])
        gate_rows[b] = gate_column(pick, gates_ref[b])
        picks.append(pick.astype(low))
        rows_v[b] = dot(picks[b], g_ref[b]).astype(low)
    streams.send_rows()
    for e in range(experts):
        at = slice(e * CAP, (e + 1) * CAP)
        for i, group in enumerate(streams.groups):
            if e == group.start:
                streams.wait_weights(i)
        pulled = dot(rows_v[:, at, :].reshape(depth, width), down_w[e])
        gate_pre, up_pre = pre_ref[e, :, :hidden], pre_ref[e, :, hidden:]
        sigmoid = jax.nn.sigmoid(gate_pre)
        silu = gate_pre * sigmoid
        inner = (silu * up_pre).astype(low).astype(wide)
        grad_rows[:, at, :] = jnp.sum(inner * pulled, axis=1, keepdims=True).reshape(
            chunk, CAP, 1
        )
        grad_inner = pulled * gate_rows[:, at, :].reshape(depth, 1)
        dgate = (grad_inner * up_pre * sigmoid * (1.0 + gate_pre * (1.0 - sigmoid))).astype(low)
        dup = (grad_inner * silu).astype(low)
        dgate_ref[e] = dgate
        dup_ref[e] = dup
        out = dot(jnp.concatenate([dgate, dup], axis=1), joint_w[e]).astype(low)
        out_v[:, at, :] = out.reshape(chunk, CAP, width)
    for b in range(chunk):
        write_parts(x_refs, b, dot(picks[b], out_v[b], tn_dims).astype(low))
        per_row = picks[b].astype(wide) * grad_rows[b]
        grads_ref[b] = jnp.sum(per_row.reshape(experts, CAP, tokens), axis=1)
    streams.end()


class Experts:
    def __init__(self, blocks, chunk, tokens, width, experts, hidden):
        self.chunk, self.half = chunk, blocks // 2
        self.tokens, self.width, self.experts, self.hidden = tokens, width, experts, hidden
        self.rows = blocks * CAP

    def mine(self, first, *shape):
        return pl.BlockSpec(
            (self.chunk,) + shape,
            lambda i, core: (2 * (i + first) + core[0],) + (0,) * len(shape),
        )

    def listed(self, first, *shape):
        return pl.BlockSpec(
            (self.chunk,) + shape, lambda i, core: (i + first,) + (0,) * len(shape)
        )

    def by_row(self, last, first):
        return pl.BlockSpec(
            (self.experts, self.chunk * CAP, last), lambda i, core: (0, i + first, 0)
        )

    def call(self, kernel, name, first, count, turn, parts, core, ins, in_specs, outs, given):
        any_spec = pl.BlockSpec(memory_space=pl.ANY)
        base = turn * self.half + first * self.chunk
        joint = [self.experts, self.width, self.width]
        joint[2 if kernel is forward_kernel else 1] = 2 * self.hidden
        given = [None] * (len(outs) - len(given)) + given
        goes_on = [i for i, array in enumerate(given) if array is not None]
        rows = self.experts * count * self.chunk * CAP
        results = pl.pallas_call(
            functools.partial(kernel, base, len(goes_on), parts),
            grid_spec=pltpu.PrefetchScalarGridSpec(
                num_scalar_prefetch=1,
                grid=(count,),
                in_specs=in_specs + [any_spec] * (3 + len(goes_on)),
                out_specs=[spec or any_spec for _, _, spec in outs],
                scratch_shapes=[pltpu.VMEM(tuple(joint), low), pltpu.VMEM(ins[-1].shape, low)]
                + [pltpu.VMEM((self.chunk, self.experts * CAP, self.width), low)] * 2
                + [pltpu.VMEM((self.chunk, self.experts * CAP, 1), wide)] * (1 if kernel is forward_kernel else 2)
                + [
                    pltpu.SemaphoreType.DMA((3, self.experts)),
                    pltpu.SemaphoreType.DMA((self.experts,)),
                ],
            ),
            out_shape=[jax.ShapeDtypeStruct(shape, kind) for shape, kind, _ in outs],
            input_output_aliases={1 + len(ins) + n: i for n, i in enumerate(goes_on)},
            compiler_params=pltpu.CompilerParams(
                dimension_semantics=("arbitrary",), vmem_limit_bytes=60 * 1024 * 1024
            ),
            cost_estimate=pl.CostEstimate(
                flops=10 * rows * self.width * (3 * self.hidden + 256),
                bytes_accessed=rows * self.width * 8,
                transcendentals=0,
            ),
            name=name,
        )(core, *ins, *(given[i] for i in goes_on))
        return list(results)

    def token_outs(self, first, parts):
        share = self.tokens // parts
        part = ((self.half, share, self.width), low, self.listed(first, share, self.width))
        by_token = (
            (self.half, self.experts, self.tokens),
            wide,
            self.listed(first, self.experts, self.tokens),
        )
        return [part] * parts + [by_token]

    def row_out(self, first, turn):
        first += turn * self.half // self.chunk
        return (
            (self.experts, self.rows, self.hidden),
            low,
            self.by_row(self.hidden, first),
        )

    def taken(self):
        return ((self.experts, self.rows // CAP, CAP, self.width), low, None)

    def forward(self, first, count, turn, parts, core, slots, router, tokens, weights, given):
        pre = (
            (self.experts, self.half * CAP, 2 * self.hidden),
            wide,
            self.by_row(2 * self.hidden, first),
        )
        return self.call(
            forward_kernel,
            "experts_forward",
            first,
            count,
            turn,
            parts,
            core,
            (slots, router, tokens, *weights),
            [
                self.mine(first, self.experts, self.tokens),
                pl.BlockSpec(router.shape, lambda i, core: (0, 0)),
                self.mine(first, self.tokens, self.width),
            ],
            self.token_outs(first, parts) + [pre, self.row_out(first, turn), self.taken()],
            given,
        )

    def backward(
        self, first, count, turn, parts, core, slots, gates, grads, pre, weights, given
    ):
        return self.call(
            backward_kernel,
            "experts_backward",
            first,
            count,
            turn,
            parts,
            core,
            (slots, gates, grads, pre, *weights),
            [
                self.mine(first, self.experts, self.tokens),
                self.listed(first, self.experts, self.tokens),
                self.mine(first, self.tokens, self.width),
                self.by_row(2 * self.hidden, first),
            ],
            self.token_outs(first, parts)
            + [self.row_out(first, turn), self.row_out(first, turn), self.taken()],
            given,
        )


def on_device(
    hidden_in,
    w_query,
    w_key,
    w_value,
    w_output,
    w_router,
    gain_attn,
    gain_ffn,
    gain_query,
    gain_key,
    w_gate,
    w_up,
    w_down,
    expert_ids,
    grad_out,
):
    tokens_dev, model_width = hidden_in.shape
    local_experts, _, hidden_units = w_gate.shape
    expert_count = w_router.shape[1]
    grid = Grid()
    blocks = grid.ep * grid.tp
    weight_rows = model_width // blocks
    both = ("ep", "tp")
    inv_root = 1.0 / math.sqrt(HEAD_DIM)

    def gathered(values):
        return lax.all_gather(values, both, axis=0, tiled=True)

    named = jnp.any(
        expert_ids[None, :, :] == jnp.arange(expert_count, dtype=jnp.int32)[:, None, None], axis=2
    )
    before = (jnp.arange(tokens_dev)[:, None] <= jnp.arange(tokens_dev)[None, :]).astype(low)
    counted = jnp.dot(named.astype(low), before, preferred_element_type=wide)
    slots = jnp.where(named, counted, 0.0).astype(low)

    shared = jnp.concatenate(
        [
            w_router,
            jnp.stack([gain_attn, gain_ffn, gain_query, gain_key], axis=1),
            jnp.zeros((w_router.shape[0], tokens_dev - expert_count - 4), low),
        ],
        axis=1,
    )
    small_all = grid.gather(jnp.concatenate([shared, slots], axis=0), "xyuwc")
    projections = gathered(jnp.concatenate([w_query, w_key, w_value], axis=1))
    projections, output_full, small_all = together(
        projections, grid.gather_rows(w_output), small_all
    )
    upstream_all = gathered(after(grad_out, projections)[None])
    small_all = small_all.reshape(blocks, weight_rows + expert_count, tokens_dev)
    shared_full = small_all[:, :weight_rows].reshape(model_width, tokens_dev)
    slots_all = small_all[:, weight_rows:]
    router_full = shared_full[:, :expert_count]
    gains = shared_full[:, expert_count : expert_count + 4].astype(wide).T
    attn_gain, ffn_gain, query_gain, key_gain = gains[0], gains[1], gains[2], gains[3]

    inputs_full = hidden_in.astype(wide)
    scale_attn = lax.rsqrt(jnp.mean(inputs_full * inputs_full, axis=-1, keepdims=True) + epsilon)
    unit_attn = inputs_full * scale_attn
    normed_attn = (unit_attn * attn_gain).astype(low)
    projected = jnp.dot(normed_attn, projections, preferred_element_type=wide)
    query_raw = projected[:, :model_width]
    key_raw = projected[:, model_width : 2 * model_width]
    value_raw = projected[:, 2 * model_width :]
    scale_query = lax.rsqrt(jnp.mean(query_raw * query_raw, axis=-1, keepdims=True) + epsilon)
    unit_query = query_raw * scale_query
    scale_key = lax.rsqrt(jnp.mean(key_raw * key_raw, axis=-1, keepdims=True) + epsilon)
    unit_key = key_raw * scale_key
    cosines, sines = rope_tables(tokens_dev, HEAD_DIM)
    query_rot = rotate(
        (unit_query * query_gain).reshape(tokens_dev, HEADS, HEAD_DIM), cosines, sines
    ).astype(low)
    key_rot = rotate(
        (unit_key * key_gain).reshape(tokens_dev, HEADS, HEAD_DIM), cosines, sines
    ).astype(low)
    value_heads = value_raw.astype(low).reshape(tokens_dev, HEADS, HEAD_DIM)
    causal = jnp.arange(tokens_dev)[:, None] >= jnp.arange(tokens_dev)[None, :]
    scores = (
        jnp.einsum("qhd,khd->hqk", query_rot, key_rot, preferred_element_type=wide) * inv_root
    )
    scores = jnp.where(causal[None], scores, masked_value)
    exponent = jnp.exp(scores - jnp.max(scores, axis=-1, keepdims=True))
    att_probs = exponent / jnp.sum(exponent, axis=-1, keepdims=True)
    probs_low = att_probs.astype(low)
    attended = (
        jnp.einsum("hqk,khd->qhd", probs_low, value_heads, preferred_element_type=wide)
        .reshape(tokens_dev, model_width)
        .astype(low)
    )
    mixed = inputs_full + jnp.dot(attended, output_full, preferred_element_type=wide)
    scale_ffn = lax.rsqrt(jnp.mean(mixed * mixed, axis=-1, keepdims=True) + epsilon)
    unit_ffn = mixed * scale_ffn
    normed_ffn = (unit_ffn * ffn_gain).astype(low)
    normed_all = gathered(normed_ffn[None])
    router_probs = jax.nn.softmax(
        jnp.dot(normed_ffn, router_full, preferred_element_type=wide), axis=-1
    )

    turned = [weights.transpose(0, 2, 1) for weights in (w_gate, w_up, w_down)]
    normed_all, turned = together(normed_all, turned)

    first_expert = lax.axis_index("ep") * local_experts
    slots_here = lax.dynamic_slice_in_dim(slots_all, first_expert, local_experts, 1).astype(wide)
    router_turned = lax.dynamic_slice_in_dim(
        jnp.concatenate([router_full, router_full], axis=1), first_expert, expert_count, 1
    )
    experts = Experts(
        blocks, grid.tp, tokens_dev, model_width, local_experts, hidden_units
    )
    core = grid.place("c")
    turns = (jnp.reshape(1 - core, (1,)), jnp.reshape(core, (1,)))
    chips = grid.chips()

    def token_sums(away, kept):
        share = tokens_dev // len(kept)
        away = away.reshape(chips + away.shape[1:])
        return [
            (part.reshape(chips + part.shape[1:]), away[..., i * share : (i + 1) * share, :])
            for i, part in enumerate(kept)
        ]

    groups = blocks // 2 // grid.tp
    part = groups // 2
    forward_ins = (slots_here, router_turned, normed_all, (w_gate, w_up, w_down))
    y_ahead, gates_ahead, pre_ahead, *given = experts.forward(
        0, groups, 0, 1, turns[0], *forward_ins, []
    )
    *y_own, gates_own, pre_own, inner_scaled, rows_in = experts.forward(
        0, groups, 1, 2, turns[1], *forward_ins, given
    )
    y_away = grid.shift(y_ahead, "c", 1)
    y_own, y_away, gates_own, slots_here = together(y_own, y_away, gates_own, slots_here)
    expert_sums = token_sums(y_away, y_own)

    def backward(first, count, turn, parts, gates, pre, given):
        return experts.backward(
            first,
            count,
            turn,
            parts,
            turns[turn],
            slots_here,
            gates,
            upstream_all,
            pre,
            turned,
            given,
        )

    def by_core(values):
        values = values.reshape(tokens_dev, chips[0] * chips[1], 2, -1)
        return [
            lax.dynamic_index_in_dim(values, at, 2, keepdims=False).reshape(tokens_dev, -1)
            for at in (1 - core, core)
        ]

    away, kept = (
        jnp.concatenate(cut, axis=1)
        for cut in zip(by_core(normed_attn), by_core(attended), strict=True)
    )
    ahead = backward(0, groups, 0, 1, gates_ahead, pre_ahead, [])
    expert_sums = grid.reduce_first(expert_sums)
    (x_ahead, gate_grads_ahead, *given), expert_sums, slots_here = together(
        ahead, expert_sums, slots_here
    )
    x_away = grid.shift(x_ahead, "c", 1)
    given = backward(0, part, 1, 4, gates_own, pre_own, given)
    expert_sum = grid.reduce_second(expert_sums, 0)
    pair_rows = jnp.concatenate([kept, grid.shift(away, "c", 1)], axis=0)
    given, expert_sum, x_away, slots_here, pair_rows = together(
        given, expert_sum, x_away, slots_here, pair_rows
    )
    own = backward(part, groups - part, 1, 4, gates_own, pre_own, given)
    expert_sum = grid.reduce_axis(expert_sum, "w", "uw")
    half = model_width // 2
    x_rows = jnp.concatenate(grid.from_line(pair_rows, "x"), axis=0)
    y_rows = jnp.concatenate(grid.from_line(pair_rows[:, :half], "y"), axis=0)
    own, expert_sum, x_rows, y_rows = together(own, expert_sum, x_rows, y_rows)
    *x_own, gate_grads_own, grad_gate_part, grad_up_part, rows_up = own
    rows_in = rows_in.reshape(local_experts, -1, model_width)
    rows_up = rows_up.reshape(local_experts, -1, model_width)

    def weight_grad(subscripts, left, right):
        return jnp.einsum(subscripts, left, right, preferred_element_type=wide)

    x_own, x_away, rows_in, rows_up, inner_scaled, expert_sum = together(
        x_own, x_away, rows_in, rows_up, inner_scaled, expert_sum
    )
    sums = token_sums(x_away, x_own)
    acc_gate = weight_grad("erd,erh->edh", rows_in, grad_gate_part)
    early = grid.reduce_first(sums[:2])
    expert_sum = grid.reduce_axis(expert_sum, "u", "u")
    gate_grads = jnp.stack([gate_grads_own, gate_grads_ahead])
    early, late, acc_gate, expert_sum, rows_in, rows_up, gate_grads = together(
        early, sums[2:], acc_gate, expert_sum, rows_in, rows_up, gate_grads
    )
    acc_down = weight_grad("erh,erd->ehd", inner_scaled, rows_up)
    early = grid.reduce_second(early, 0)
    late = grid.reduce_first(late)
    early, late, acc_down, rows_in = together(early, late, acc_down, rows_in)
    acc_up = weight_grad("erd,erh->edh", rows_in, grad_up_part)
    early = grid.reduce_axis(early, "w", "uw")
    late = grid.reduce_second(late, 0)
    early, late, acc_up = together(early, late, acc_up)
    early = grid.reduce_axis(early, "u", "u")
    late = grid.reduce_axis(late, "w", "uw")
    early, late = together(early, late)
    late = grid.reduce_axis(late, "u", "u")
    block_out = (mixed + expert_sum.astype(wide)).astype(low)

    gate_grads = jnp.where(core == 0, gate_grads, gate_grads[::-1])
    gate_grads = gate_grads.reshape((2,) + chips + (local_experts, tokens_dev))
    gate_grads = grid.reduce_scatter(gate_grads, "wu", "cyxuw")
    gate_grads = lax.dynamic_update_slice_in_dim(
        jnp.zeros(gate_grads.shape[:3] + (expert_count, tokens_dev), wide),
        gate_grads,
        first_expert,
        3,
    )
    grad_probs = grid.reduce_scatter(gate_grads, "cyx", "cyx").T
    back_sum, block_out, acc_gate, acc_up, acc_down = together(
        jnp.concatenate([early, late], axis=0), block_out, acc_gate, acc_up, acc_down
    )

    upstream = grad_out.astype(wide)
    grad_logits = router_probs * (
        grad_probs - jnp.sum(router_probs * grad_probs, axis=-1, keepdims=True)
    )
    grad_ffn_normed = back_sum.astype(wide) + jnp.dot(
        grad_logits, router_full.astype(wide).T, precision=lax.Precision.HIGHEST
    )
    grad_router_local = jnp.dot(
        normed_ffn.astype(wide).T, grad_logits, precision=lax.Precision.HIGHEST
    )
    grad_ffn_gain = jnp.sum(grad_ffn_normed * unit_ffn, axis=0)
    grad_mixed = upstream + rms_back(grad_ffn_normed, unit_ffn, ffn_gain, scale_ffn)
    grad_branch = grad_mixed.astype(low)

    output_columns = grid.columns_from_line(grad_branch, "x")
    grad_attended = jnp.einsum(
        "te,de->td", grad_branch, output_full, preferred_element_type=wide
    ).astype(low)
    grad_heads = grad_attended.reshape(tokens_dev, HEADS, HEAD_DIM)
    grad_value_rows = (
        jnp.einsum("hqk,qhd->khd", probs_low, grad_heads, preferred_element_type=wide)
        .reshape(tokens_dev, model_width)
        .astype(low)
    )
    value_columns = grid.columns_from_line(grad_value_rows, "y")
    grad_probs_att = jnp.einsum(
        "qhd,khd->hqk", grad_heads, value_heads, preferred_element_type=wide
    )
    grad_scores = (
        att_probs * (grad_probs_att - jnp.sum(att_probs * grad_probs_att, axis=-1, keepdims=True))
    ).astype(low)
    grad_qrot = (
        jnp.einsum("hqk,khd->qhd", grad_scores, key_rot, preferred_element_type=wide) * inv_root
    )
    grad_krot = (
        jnp.einsum("hqk,qhd->khd", grad_scores, query_rot, preferred_element_type=wide) * inv_root
    )
    grad_qnorm = unrotate(bounce(grad_qrot), cosines, sines).reshape(tokens_dev, model_width)
    grad_knorm = unrotate(bounce(grad_krot), cosines, sines).reshape(tokens_dev, model_width)
    grad_query_gain = jnp.sum(grad_qnorm * unit_query, axis=0)
    grad_key_gain = jnp.sum(grad_knorm * unit_key, axis=0)
    grad_query_raw = rms_back(grad_qnorm, unit_query, query_gain, scale_query).astype(low)
    grad_key_raw = rms_back(grad_knorm, unit_key, key_gain, scale_key).astype(low)
    output_columns, value_columns, grad_query_raw, grad_key_raw = together(
        output_columns, value_columns, grad_query_raw, grad_key_raw
    )

    def outer(left, right):
        total = jnp.einsum("tc,te->ce", left, right, preferred_element_type=wide)
        return total.astype(low).reshape(chips + (weight_rows, -1))

    first = [outer(x_rows[:, half:], output_columns), outer(y_rows, value_columns)]
    second = [
        grid.columns_from_line(grad_query_raw, "x"),
        grid.columns_from_line(grad_key_raw, "y"),
    ]
    first, second = together(first, second)
    first = grid.reduce_first(first)
    second = [outer(x_rows[:, :half], second[0]), outer(y_rows, second[1])]
    grads = jnp.concatenate([grad_query_raw, grad_key_raw, grad_value_rows], axis=1)
    grad_attn_normed = jnp.einsum("te,ce->tc", grads, projections, preferred_element_type=wide)
    grad_attn_gain = jnp.sum(grad_attn_normed * unit_attn, axis=0)
    grad_input = grad_mixed + rms_back(grad_attn_normed, unit_attn, attn_gain, scale_attn)
    gain_sums = jnp.stack(
        [grad_attn_gain, grad_ffn_gain, grad_query_gain, grad_key_gain], axis=1
    )
    small_sums = jnp.concatenate([grad_router_local, gain_sums], axis=1).reshape(
        grid.shape + (weight_rows, expert_count + gain_sums.shape[1])
    )
    first, second, small_sums, grad_input = together(first, second, small_sums, grad_input)
    first = grid.reduce_both(first, "w")
    second = grid.reduce_first(second)
    small_sums = grid.reduce_scatter(small_sums, "c")
    first, second, small_sums = together(first, second, small_sums)
    first = grid.reduce_both(first, "u")
    second = grid.reduce_both(second, "w")
    small_sums = grid.reduce_scatter(small_sums, "y", "yxuw")
    first, second, small_sums = together(first, second, small_sums)
    grad_output, grad_value = grid.rows_of_both(first)
    second = grid.reduce_both(second, "u")
    small_sums = grid.reduce_scatter(small_sums, "x", "xuw")
    grad_output, grad_value, second, small_sums = together(
        grad_output, grad_value, second, small_sums
    )
    grad_query, grad_key = grid.rows_of_both(second)
    small_sums = grid.reduce_scatter(small_sums, "wu", "uw")
    grad_query, grad_key, grad_value, grad_output = (
        grad.astype(wide) for grad in (grad_query, grad_key, grad_value, grad_output)
    )
    return (
        block_out,
        grad_input,
        grad_query,
        grad_key,
        grad_value,
        grad_output,
        small_sums[:, :expert_count],
        *(small_sums[:, expert_count + i] for i in range(4)),
        acc_gate,
        acc_up,
        acc_down,
    )


def solution(mesh):
    placed = (
        P(("ep", "tp"), None),
        P(("ep", "tp"), None),
        P(("ep", "tp"), None),
        P(("ep", "tp"), None),
        P(("ep", "tp"), None),
        P(("ep", "tp"), None),
        P(("ep", "tp")),
        P(("ep", "tp")),
        P(("ep", "tp")),
        P(("ep", "tp")),
        P("ep", None, "tp"),
        P("ep", None, "tp"),
        P("ep", "tp", None),
        P(("ep", "tp"), None),
        P(("ep", "tp"), None),
    )
    return jax.shard_map(
        on_device,
        mesh=mesh,
        in_specs=placed,
        out_specs=(
            P(("ep", "tp"), None),
            P(("ep", "tp"), None),
            P(("ep", "tp"), None),
            P(("ep", "tp"), None),
            P(("ep", "tp"), None),
            P(("ep", "tp"), None),
            P(("ep", "tp"), None),
            P(("ep", "tp")),
            P(("ep", "tp")),
            P(("ep", "tp")),
            P(("ep", "tp")),
            P("ep", None, "tp"),
            P("ep", None, "tp"),
            P("ep", "tp", None),
        ),
        check_vma=False,
    )
```

```python
import functools
import math

import jax
import jax.numpy as jnp
from jax import lax
from jax.experimental import pallas as pl
from jax.experimental.pallas import tpu as pltpu
from jax.sharding import PartitionSpec as P

HEADS = 16
HEAD_DIM = 128
CAP = 32


epsilon = 1e-05
rope_base = 10000.0
masked_value = -1e30
low = jnp.bfloat16
wide = jnp.float32


def rope_tables(length, head_dim):
    half_dim = head_dim // 2
    position = jnp.arange(length, dtype=jnp.float32)
    frequency = jnp.exp(
        jnp.arange(half_dim, dtype=jnp.float32) * (-2.0 * math.log(rope_base) / head_dim)
    )
    angles = position[:, None] * frequency[None, :]
    return (jnp.cos(angles)[:, None, :], jnp.sin(angles)[:, None, :])


def rotate(values, cosines, sines):
    half_dim = values.shape[-1] // 2
    first_half = values[..., :half_dim]
    second = values[..., half_dim:]
    return jnp.concatenate(
        [first_half * cosines - second * sines, second * cosines + first_half * sines], axis=-1
    )


def unrotate(grad_vals, cosines, sines):
    half_dim = grad_vals.shape[-1] // 2
    first_half = grad_vals[..., :half_dim]
    second = grad_vals[..., half_dim:]
    return jnp.concatenate(
        [first_half * cosines + second * sines, second * cosines - first_half * sines], axis=-1
    )


def rms_back(grad_normed, unit_vals, gain_vals, inv_scale):
    scaled = grad_normed * gain_vals
    return inv_scale * (scaled - unit_vals * jnp.mean(scaled * unit_vals, axis=-1, keepdims=True))


def bounce(values):
    return lax.optimization_barrier(values.astype(low)).astype(wide)


def after(values, *needs):
    return lax.optimization_barrier((values, needs))[0]


def together(*values):
    return lax.optimization_barrier(values)


def chosen(index, cases):
    return lax.select_n(index.astype(jnp.int32), *cases)


class Grid:
    axes = "yxcuw"

    def __init__(self):
        self.ep, self.tp = lax.axis_size("ep"), lax.axis_size("tp")
        chips = self.ep // 2
        nx = math.isqrt(chips)
        while chips % nx:
            nx -= 1
        nw = 2 - self.tp % 2
        self.size = {"y": chips // nx, "x": nx, "c": 2, "u": self.tp // nw, "w": nw, "z": self.tp}
        self.stride = {"y": 2 * nx, "x": 2, "c": 1, "u": nw, "w": 1, "z": 1}
        self.shape = tuple(self.size[axis] for axis in self.axes)

    def place(self, axis):
        whole = lax.axis_index("tp" if axis in "uwz" else "ep")
        return whole // self.stride[axis] % self.size[axis]

    def shift(self, values, axis, step):
        count, stride = self.size[axis], self.stride[axis]
        pairs = []
        for i in range(self.tp if axis in "uwz" else self.ep):
            own = i // stride % count
            pairs.append((i, i + ((own + step) % count - own) * stride))
        return lax.ppermute(values, "tp" if axis in "uwz" else "ep", pairs)

    def gather_axis(self, values, axis):
        dim, count, own = self.axes.index(axis), self.size[axis], self.place(axis)
        parts = [values] + [self.shift(values, axis, step) for step in range(1, count)]
        shape = list(values.shape)
        shape[dim] = count
        values = jnp.zeros(shape, values.dtype)
        for step, part in enumerate(parts):
            values = lax.dynamic_update_slice_in_dim(values, part, (own - step) % count, dim)
        return values

    def gather(self, values, order):
        values = values[(None,) * len(self.axes)]
        for axis in order:
            values = self.gather_axis(values, axis)
        return values

    def gather_first(self, values):
        rows = values.shape[0]
        values = self.gather(values, "uw")
        halves = values[..., : rows // 2, :], values[..., rows // 2 :, :]
        return [self.gather_axis(half, axis) for half, axis in zip(halves, "xy", strict=True)]

    def gather_second(self, halves):
        halves = [self.gather_axis(half, axis) for half, axis in zip(halves, "yx", strict=True)]
        values = self.gather_axis(jnp.concatenate(halves, axis=-2), "c")
        return values.reshape(-1, values.shape[-1])

    def reduce_axis(self, values, axis, axes):
        dim, count, own = axes.index(axis), self.size[axis], self.place(axis)
        values = values if isinstance(values, (list, tuple)) else [values]
        kind = values[0].dtype

        def part(step):
            return sum(
                lax.dynamic_index_in_dim(v, (own - step) % count, dim, keepdims=False).astype(wide)
                for v in values
            )

        total = part(0)
        for step in range(1, count):
            total = total + self.shift(part(step).astype(kind), axis, -step).astype(wide)
        return total.astype(kind)

    def reduce_scatter(self, values, order, axes=axes):
        for axis in order:
            values = self.reduce_axis(values, axis, axes)
            axes = axes.replace(axis, "")
        return values

    def from_line(self, values, axis):
        return [values] + [
            self.shift(values, axis, step) for step in range(1, self.size[axis])
        ]

    def columns_from_line(self, values, axis):
        count, own = self.size[axis], self.place(axis)
        parts = jnp.split(values, count, axis=1)
        taken = [chosen(own, parts)]
        for step in range(1, count):
            taken.append(self.shift(chosen((own + step) % count, parts), axis, step))
        taken = jnp.stack(taken)
        taken = jnp.stack([taken, self.shift(taken, "c", 1)], axis=1)
        return taken.reshape(-1, taken.shape[-1])

    def rows_from_line(self, values, axis):
        count, own = self.size[axis], self.place(axis)
        got = [chosen(own, list(values))]
        for step in range(1, count):
            got.append(self.shift(chosen((own + step) % count, list(values)), axis, step))
        return jnp.concatenate(
            [chosen((own - j) % count, got) for j in range(count)], axis=1
        ).astype(wide)

    def reduce_first(self, pair):
        return [self.reduce_axis(v, axis, "yxuw") for v, axis in zip(pair, "yx", strict=True)]

    def alike(self, pair):
        return jnp.stack(pair) if self.size["y"] == self.size["x"] else pair

    def reduce_both(self, pair, axis):
        left = "uw" if axis == "w" else "u"
        if isinstance(pair, list):
            return [
                self.reduce_axis(v, axis, line + left) for v, line in zip(pair, "xy", strict=True)
            ]
        return self.reduce_axis(pair, axis, "pl" + left)

    def rows_of_both(self, pair):
        return [self.rows_from_line(v, line) for v, line in zip(pair, "xy", strict=True)]

    def reduce_second(self, pair, join):
        pair = [
            self.reduce_axis(v, axis, axis + "uw") for v, axis in zip(pair, "xy", strict=True)
        ]
        return jnp.concatenate(pair, axis=join + 2)

    def chips(self):
        return tuple(self.size[axis] for axis in "yxuw")


nt_dims = (((1,), (1,)), ((), ()))
tn_dims = (((0,), (0,)), ((), ()))


def one_hot(slots):
    experts, tokens = slots.shape
    place = lax.broadcasted_iota(jnp.int32, (experts, CAP, tokens), 1).astype(wide) + 1.0
    return (slots[:, None, :] == place).astype(wide).reshape(experts * CAP, tokens)


def dot(left, right, dims=(((1,), (0,)), ((), ()))):
    return lax.dot_general(left, right, dims, preferred_element_type=wide)


def gate_column(pick, gates):
    spread = jnp.broadcast_to(gates[:, None, :], (gates.shape[0], CAP, gates.shape[1]))
    return jnp.sum(pick * spread.reshape(pick.shape), axis=1, keepdims=True)


def product_kernel(left_ref, right_ref, out_ref):
    out_ref[...] = dot(left_ref[...], right_ref[...], nt_dims)


def turned_product(left, right, block=256):
    rows, depth = left.shape
    columns = right.shape[0]
    return pl.pallas_call(
        product_kernel,
        grid=(columns // block,),
        in_specs=[
            pl.BlockSpec((rows, depth), lambda i: (0, 0)),
            pl.BlockSpec((block, depth), lambda i: (i, 0)),
        ],
        out_specs=pl.BlockSpec((rows, block), lambda i: (0, i)),
        out_shape=jax.ShapeDtypeStruct((rows, columns), wide),
        compiler_params=pltpu.CompilerParams(vmem_limit_bytes=40 * 1024 * 1024),
        cost_estimate=pl.CostEstimate(
            flops=50 * rows * depth * columns, bytes_accessed=columns * depth * 2, transcendentals=0
        ),
        name="turned_product",
    )(left, right)


class Streams:
    def __init__(self, sources, targets, sems, rows_v, rows_hbm, row_sem, base):
        self.step, chunk = pl.program_id(0), rows_v.shape[0]
        experts = sources[0].shape[0]
        self.groups = [range(experts // 2), range(experts // 2, experts)]
        self.weights = [
            [
                pltpu.make_async_copy(source.at[e], target(e), sems.at[i, e])
                for i, (source, target) in enumerate(zip(sources, targets, strict=True))
                for e in group
            ]
            for group in self.groups
        ]
        block = base + self.step * chunk
        self.rows = [
            pltpu.make_async_copy(
                rows_v.at[:, e * CAP : (e + 1) * CAP, :],
                rows_hbm.at[e, pl.ds(block, chunk)],
                row_sem.at[e],
            )
            for e in range(experts)
        ]

        @pl.when(self.step == 0)
        def _():
            for copies in self.weights:
                for copy in copies:
                    copy.start()

        @pl.when(self.step > 0)
        def _():
            self.wait_rows()

    def wait_rows(self):
        for copy in self.rows:
            copy.wait()

    def send_rows(self):
        for copy in self.rows:
            copy.start()

    def wait_weights(self, group):
        @pl.when(self.step == 0)
        def _():
            for copy in self.weights[group]:
                copy.wait()

    def end(self):
        @pl.when(self.step == pl.num_programs(0) - 1)
        def _():
            self.wait_rows()


def write_parts(targets, block, total):
    share = total.shape[0] // len(targets)
    for i, target in enumerate(targets):
        target[block] = total[i * share : (i + 1) * share]


def forward_kernel(base, kept, parts, _, slots_ref, router_ref, x_ref, *refs):
    weights, refs = refs[:3], refs[3:]
    refs = refs[kept:]
    y_refs, refs = refs[:parts], refs[parts:]
    gates_ref, pre_ref, inner_ref, rows_hbm = refs[:4]
    joint_w, down_w, rows_v, out_v, gate_rows, w_sems, row_sems = refs[4:]
    chunk, _, width = x_ref.shape
    experts, hidden, _ = down_w.shape
    depth = chunk * CAP
    targets = (
        lambda e: joint_w.at[e, :, :hidden],
        lambda e: joint_w.at[e, :, hidden:],
        lambda e: down_w.at[e],
    )
    streams = Streams(weights, targets, w_sems, rows_v, rows_hbm, row_sems, base)
    picks = []
    for b in range(chunk):
        tokens = x_ref[b]
        logits = dot(tokens, router_ref[...]).T
        exponent = jnp.exp(logits - jnp.max(logits, axis=0, keepdims=True))
        gates = (exponent / jnp.sum(exponent, axis=0, keepdims=True))[:experts]
        gates_ref[b] = gates
        pick = one_hot(slots_ref[b])
        gate_rows[b] = gate_column(pick, gates)
        picks.append(pick.astype(low))
        rows_v[b] = dot(picks[b], tokens).astype(low)
    streams.send_rows()
    for e in range(experts):
        at = slice(e * CAP, (e + 1) * CAP)
        for i, group in enumerate(streams.groups):
            if e == group.start:
                streams.wait_weights(i)
        pre = dot(rows_v[:, at, :].reshape(depth, width), joint_w[e])
        pre_ref[e] = pre
        gate_pre, up_pre = pre[:, :hidden], pre[:, hidden:]
        inner = (gate_pre * jax.nn.sigmoid(gate_pre) * up_pre).astype(low).astype(wide)
        scaled = (inner * gate_rows[:, at, :].reshape(depth, 1)).astype(low)
        inner_ref[e] = scaled
        out = dot(scaled, down_w[e]).astype(low)
        out_v[:, at, :] = out.reshape(chunk, CAP, width)
    for b in range(chunk):
        write_parts(y_refs, b, dot(picks[b], out_v[b], tn_dims).astype(low))
    streams.end()


def backward_kernel(base, kept, parts, _, slots_ref, gates_ref, g_ref, pre_ref, *refs):
    weights, refs = refs[:3], refs[3:]
    refs = refs[kept:]
    x_refs, refs = refs[:parts], refs[parts:]
    grads_ref, dgate_ref, dup_ref, rows_hbm = refs[:4]
    joint_w, down_w, rows_v, out_v, gate_rows, grad_rows, w_sems, row_sems = refs[4:]
    chunk, tokens, width = g_ref.shape
    experts, _, hidden = down_w.shape
    depth = chunk * CAP
    targets = (
        lambda e: joint_w.at[e, :hidden],
        lambda e: joint_w.at[e, hidden:],
        lambda e: down_w.at[e],
    )
    streams = Streams(weights, targets, w_sems, rows_v, rows_hbm, row_sems, base)
    picks = []
    for b in range(chunk):
        pick = one_hot(slots_ref[b])
        gate_rows[b] = gate_column(pick, gates_ref[b])
        picks.append(pick.astype(low))
        rows_v[b] = dot(picks[b], g_ref[b]).astype(low)
    streams.send_rows()
    for e in range(experts):
        at = slice(e * CAP, (e + 1) * CAP)
        for i, group in enumerate(streams.groups):
            if e == group.start:
                streams.wait_weights(i)
        pulled = dot(rows_v[:, at, :].reshape(depth, width), down_w[e])
        gate_pre, up_pre = pre_ref[e, :, :hidden], pre_ref[e, :, hidden:]
        sigmoid = jax.nn.sigmoid(gate_pre)
        silu = gate_pre * sigmoid
        inner = (silu * up_pre).astype(low).astype(wide)
        grad_rows[:, at, :] = jnp.sum(inner * pulled, axis=1, keepdims=True).reshape(
            chunk, CAP, 1
        )
        grad_inner = pulled * gate_rows[:, at, :].reshape(depth, 1)
        dgate = (grad_inner * up_pre * sigmoid * (1.0 + gate_pre * (1.0 - sigmoid))).astype(low)
        dup = (grad_inner * silu).astype(low)
        dgate_ref[e] = dgate
        dup_ref[e] = dup
        out = dot(jnp.concatenate([dgate, dup], axis=1), joint_w[e]).astype(low)
        out_v[:, at, :] = out.reshape(chunk, CAP, width)
    for b in range(chunk):
        write_parts(x_refs, b, dot(picks[b], out_v[b], tn_dims).astype(low))
        per_row = picks[b].astype(wide) * grad_rows[b]
        grads_ref[b] = jnp.sum(per_row.reshape(experts, CAP, tokens), axis=1)
    streams.end()


class Experts:
    def __init__(self, blocks, chunk, tokens, width, experts, hidden):
        self.chunk, self.half = chunk, blocks // 2
        self.tokens, self.width, self.experts, self.hidden = tokens, width, experts, hidden
        self.rows = blocks * CAP

    def mine(self, first, *shape):
        return pl.BlockSpec(
            (self.chunk,) + shape,
            lambda i, core: (2 * (i + first) + core[0],) + (0,) * len(shape),
        )

    def listed(self, first, *shape):
        return pl.BlockSpec(
            (self.chunk,) + shape, lambda i, core: (i + first,) + (0,) * len(shape)
        )

    def by_row(self, last, first):
        return pl.BlockSpec(
            (self.experts, self.chunk * CAP, last), lambda i, core: (0, i + first, 0)
        )

    def call(self, kernel, name, first, count, turn, parts, core, ins, in_specs, outs, given):
        any_spec = pl.BlockSpec(memory_space=pl.ANY)
        base = turn * self.half + first * self.chunk
        joint = [self.experts, self.width, self.width]
        joint[2 if kernel is forward_kernel else 1] = 2 * self.hidden
        given = [None] * (len(outs) - len(given)) + given
        goes_on = [i for i, array in enumerate(given) if array is not None]
        rows = self.experts * count * self.chunk * CAP
        results = pl.pallas_call(
            functools.partial(kernel, base, len(goes_on), parts),
            grid_spec=pltpu.PrefetchScalarGridSpec(
                num_scalar_prefetch=1,
                grid=(count,),
                in_specs=in_specs + [any_spec] * (3 + len(goes_on)),
                out_specs=[spec or any_spec for _, _, spec in outs],
                scratch_shapes=[pltpu.VMEM(tuple(joint), low), pltpu.VMEM(ins[-1].shape, low)]
                + [pltpu.VMEM((self.chunk, self.experts * CAP, self.width), low)] * 2
                + [pltpu.VMEM((self.chunk, self.experts * CAP, 1), wide)] * (1 if kernel is forward_kernel else 2)
                + [
                    pltpu.SemaphoreType.DMA((3, self.experts)),
                    pltpu.SemaphoreType.DMA((self.experts,)),
                ],
            ),
            out_shape=[jax.ShapeDtypeStruct(shape, kind) for shape, kind, _ in outs],
            input_output_aliases={1 + len(ins) + n: i for n, i in enumerate(goes_on)},
            compiler_params=pltpu.CompilerParams(
                dimension_semantics=("arbitrary",), vmem_limit_bytes=60 * 1024 * 1024
            ),
            cost_estimate=pl.CostEstimate(
                flops=10 * rows * self.width * (3 * self.hidden + 256),
                bytes_accessed=rows * self.width * 8,
                transcendentals=0,
            ),
            name=name,
        )(core, *ins, *(given[i] for i in goes_on))
        return list(results)

    def token_outs(self, first, parts):
        share = self.tokens // parts
        part = ((self.half, share, self.width), low, self.listed(first, share, self.width))
        by_token = (
            (self.half, self.experts, self.tokens),
            wide,
            self.listed(first, self.experts, self.tokens),
        )
        return [part] * parts + [by_token]

    def row_out(self, first, turn):
        first += turn * self.half // self.chunk
        return (
            (self.experts, self.rows, self.hidden),
            low,
            self.by_row(self.hidden, first),
        )

    def taken(self):
        return ((self.experts, self.rows // CAP, CAP, self.width), low, None)

    def forward(self, first, count, turn, parts, core, slots, router, tokens, weights, given):
        pre = (
            (self.experts, self.half * CAP, 2 * self.hidden),
            wide,
            self.by_row(2 * self.hidden, first),
        )
        return self.call(
            forward_kernel,
            "experts_forward",
            first,
            count,
            turn,
            parts,
            core,
            (slots, router, tokens, *weights),
            [
                self.mine(first, self.experts, self.tokens),
                pl.BlockSpec(router.shape, lambda i, core: (0, 0)),
                self.mine(first, self.tokens, self.width),
            ],
            self.token_outs(first, parts) + [pre, self.row_out(first, turn), self.taken()],
            given,
        )

    def backward(
        self, first, count, turn, parts, core, slots, gates, grads, pre, weights, given
    ):
        return self.call(
            backward_kernel,
            "experts_backward",
            first,
            count,
            turn,
            parts,
            core,
            (slots, gates, grads, pre, *weights),
            [
                self.mine(first, self.experts, self.tokens),
                self.listed(first, self.experts, self.tokens),
                self.mine(first, self.tokens, self.width),
                self.by_row(2 * self.hidden, first),
            ],
            self.token_outs(first, parts)
            + [self.row_out(first, turn), self.row_out(first, turn), self.taken()],
            given,
        )


def on_device(
    hidden_in,
    w_query,
    w_key,
    w_value,
    w_output,
    w_router,
    gain_attn,
    gain_ffn,
    gain_query,
    gain_key,
    w_gate,
    w_up,
    w_down,
    expert_ids,
    grad_out,
):
    tokens_dev, model_width = hidden_in.shape
    local_experts, _, hidden_units = w_gate.shape
    expert_count = w_router.shape[1]
    grid = Grid()
    blocks = grid.ep * grid.tp
    weight_rows = model_width // blocks
    both = ("ep", "tp")
    inv_root = 1.0 / math.sqrt(HEAD_DIM)

    def gathered(values):
        return lax.all_gather(values, both, axis=0, tiled=True)

    named = jnp.any(
        expert_ids[None, :, :] == jnp.arange(expert_count, dtype=jnp.int32)[:, None, None], axis=2
    )
    before = (jnp.arange(tokens_dev)[:, None] <= jnp.arange(tokens_dev)[None, :]).astype(low)
    counted = jnp.dot(named.astype(low), before, preferred_element_type=wide)
    slots = jnp.where(named, counted, 0.0).astype(low)

    shared = jnp.concatenate(
        [
            w_router,
            jnp.stack([gain_attn, gain_ffn, gain_query, gain_key], axis=1),
            jnp.zeros((w_router.shape[0], tokens_dev - expert_count - 4), low),
        ],
        axis=1,
    )
    output_full = grid.gather_second(grid.gather_first(w_output))
    small_all = after(jnp.concatenate([shared, slots], axis=0), output_full)
    small_all = grid.gather(small_all, "xyuwc")
    small_all = small_all.reshape(blocks, weight_rows + expert_count, tokens_dev)
    shared_full = small_all[:, :weight_rows].reshape(model_width, tokens_dev)
    slots_all = small_all[:, weight_rows:]
    router_full = shared_full[:, :expert_count]
    gains = shared_full[:, expert_count : expert_count + 4].astype(wide).T
    attn_gain, ffn_gain, query_gain, key_gain = gains[0], gains[1], gains[2], gains[3]

    projections = gathered(jnp.concatenate([w_query, w_key, w_value], axis=1))
    inputs_full = hidden_in.astype(wide)
    scale_attn = lax.rsqrt(jnp.mean(inputs_full * inputs_full, axis=-1, keepdims=True) + epsilon)
    unit_attn = inputs_full * scale_attn
    normed_attn = (unit_attn * attn_gain).astype(low)
    projections, output_full, normed_attn, query_gain, key_gain, ffn_gain = together(
        projections,
        output_full,
        normed_attn,
        query_gain,
        key_gain,
        ffn_gain,
    )
    upstream_all = gathered(after(grad_out, projections)[None])
    projected = jnp.dot(normed_attn, projections, preferred_element_type=wide)
    query_raw = projected[:, :model_width]
    key_raw = projected[:, model_width : 2 * model_width]
    value_raw = projected[:, 2 * model_width :]
    scale_query = lax.rsqrt(jnp.mean(query_raw * query_raw, axis=-1, keepdims=True) + epsilon)
    unit_query = query_raw * scale_query
    scale_key = lax.rsqrt(jnp.mean(key_raw * key_raw, axis=-1, keepdims=True) + epsilon)
    unit_key = key_raw * scale_key
    cosines, sines = rope_tables(tokens_dev, HEAD_DIM)
    query_rot = rotate(
        (unit_query * query_gain).reshape(tokens_dev, HEADS, HEAD_DIM), cosines, sines
    ).astype(low)
    key_rot = rotate(
        (unit_key * key_gain).reshape(tokens_dev, HEADS, HEAD_DIM), cosines, sines
    ).astype(low)
    value_heads = value_raw.astype(low).reshape(tokens_dev, HEADS, HEAD_DIM)
    causal = jnp.arange(tokens_dev)[:, None] >= jnp.arange(tokens_dev)[None, :]
    scores = (
        jnp.einsum("qhd,khd->hqk", query_rot, key_rot, preferred_element_type=wide) * inv_root
    )
    scores = jnp.where(causal[None], scores, masked_value)
    exponent = jnp.exp(scores - jnp.max(scores, axis=-1, keepdims=True))
    att_probs = exponent / jnp.sum(exponent, axis=-1, keepdims=True)
    probs_low = att_probs.astype(low)
    attended = (
        jnp.einsum("hqk,khd->qhd", probs_low, value_heads, preferred_element_type=wide)
        .reshape(tokens_dev, model_width)
        .astype(low)
    )
    mixed = inputs_full + jnp.dot(attended, output_full, preferred_element_type=wide)
    scale_ffn = lax.rsqrt(jnp.mean(mixed * mixed, axis=-1, keepdims=True) + epsilon)
    unit_ffn = mixed * scale_ffn
    normed_ffn = (unit_ffn * ffn_gain).astype(low)
    normed_all = gathered(normed_ffn[None])
    router_probs = jax.nn.softmax(
        jnp.dot(normed_ffn, router_full, preferred_element_type=wide), axis=-1
    )

    turned = [weights.transpose(0, 2, 1) for weights in (w_gate, w_up, w_down)]
    normed_all, turned = together(normed_all, turned)

    first_expert = lax.axis_index("ep") * local_experts
    slots_here = lax.dynamic_slice_in_dim(slots_all, first_expert, local_experts, 1).astype(wide)
    router_turned = lax.dynamic_slice_in_dim(
        jnp.concatenate([router_full, router_full], axis=1), first_expert, expert_count, 1
    )
    experts = Experts(
        blocks, grid.tp, tokens_dev, model_width, local_experts, hidden_units
    )
    core = grid.place("c")
    turns = (jnp.reshape(1 - core, (1,)), jnp.reshape(core, (1,)))
    chips = grid.chips()

    def token_sums(away, kept):
        share = tokens_dev // len(kept)
        away = away.reshape(chips + away.shape[1:])
        return [
            (part.reshape(chips + part.shape[1:]), away[..., i * share : (i + 1) * share, :])
            for i, part in enumerate(kept)
        ]

    groups = blocks // 2 // grid.tp
    forward_ins = (slots_here, router_turned, normed_all, (w_gate, w_up, w_down))
    y_ahead, gates_ahead, pre_ahead, *given = experts.forward(
        0, groups, 0, 1, turns[0], *forward_ins, []
    )
    *y_own, gates_own, pre_own, inner_scaled, rows_in = experts.forward(
        0, groups, 1, 2, turns[1], *forward_ins, given
    )
    y_away = grid.shift(y_ahead, "c", 1)
    y_own, y_away, gates_own, slots_here = together(y_own, y_away, gates_own, slots_here)
    expert_sums = token_sums(y_away, y_own)

    def backward(first, count, turn, parts, gates, pre, given):
        return experts.backward(
            first,
            count,
            turn,
            parts,
            turns[turn],
            slots_here,
            gates,
            upstream_all,
            pre,
            turned,
            given,
        )

    def by_core(values):
        parts = jnp.split(values, 2 * chips[0] * chips[1], axis=1)
        cut = [jnp.concatenate(parts[at::2], axis=1) for at in range(2)]
        return [chosen(at, cut) for at in (1 - core, core)]

    away, kept = (
        jnp.concatenate(cut, axis=1)
        for cut in zip(by_core(normed_attn), by_core(attended), strict=True)
    )
    ahead = backward(0, groups, 0, 1, gates_ahead, pre_ahead, [])
    expert_sums = grid.reduce_first(expert_sums)
    pair_rows = [kept, grid.shift(away, "c", 1)]
    (x_ahead, gate_grads_ahead, *given), expert_sums, slots_here, pair_rows = together(
        ahead, expert_sums, slots_here, pair_rows
    )
    x_away = grid.shift(x_ahead, "c", 1)
    own = backward(0, groups, 1, 4, gates_own, pre_own, given)
    expert_sum = grid.reduce_second(expert_sums, 0)
    own, expert_sum, x_away = together(own, expert_sum, x_away)
    *x_own, gate_grads_own, grad_gate_part, grad_up_part, rows_up = own
    rows_in = rows_in.reshape(local_experts, -1, model_width)
    rows_up = rows_up.reshape(local_experts, -1, model_width)

    def weight_grad(subscripts, left, right):
        return jnp.einsum(subscripts, left, right, preferred_element_type=wide)

    sums = token_sums(x_away, x_own)
    gate_grads = jnp.stack([gate_grads_own, gate_grads_ahead])
    gate_grads = jnp.where(core == 0, gate_grads, gate_grads[::-1])
    gate_grads = gate_grads.reshape((2,) + chips + (local_experts, tokens_dev))
    acc_gate = weight_grad("erd,erh->edh", rows_in, grad_gate_part)
    early = grid.reduce_first(sums[:2])
    expert_sum = grid.reduce_axis(expert_sum, "w", "uw")
    gate_grads = grid.reduce_axis(gate_grads, "w", "cyxuw")
    early, late, acc_gate, expert_sum, rows_in, rows_up, gate_grads = together(
        early, sums[2:], acc_gate, expert_sum, rows_in, rows_up, gate_grads
    )
    acc_down = weight_grad("erh,erd->ehd", inner_scaled, rows_up)
    early = grid.reduce_second(early, 0)
    late = grid.reduce_first(late)
    expert_sum = grid.reduce_axis(expert_sum, "u", "u")
    early, late, acc_down, rows_in, expert_sum, gate_grads = together(
        early, late, acc_down, rows_in, expert_sum, gate_grads
    )
    acc_up = weight_grad("erd,erh->edh", rows_in, grad_up_part)
    early = grid.reduce_axis(early, "w", "uw")
    late = grid.reduce_second(late, 0)
    gate_grads = grid.reduce_axis(gate_grads, "u", "cyxu")
    gate_grads = lax.dynamic_update_slice_in_dim(
        jnp.zeros(gate_grads.shape[:3] + (expert_count, tokens_dev), wide),
        gate_grads,
        first_expert,
        3,
    )
    block_out = (mixed + expert_sum.astype(wide)).astype(low)
    early, late, acc_up, gate_grads, pair_rows = together(
        early, late, acc_up, gate_grads, pair_rows
    )
    early = grid.reduce_axis(early, "u", "u")
    late = grid.reduce_axis(late, "w", "uw")
    gate_grads = grid.reduce_axis(gate_grads, "c", "cyx")
    pair_rows = jnp.concatenate(pair_rows, axis=0)
    normed_rows, attended_rows = jnp.split(pair_rows, 2, axis=1)
    y_rows = grid.from_line(normed_rows, "y")
    attended_rows = grid.from_line(attended_rows, "x")
    early, late, gate_grads, y_rows, attended_rows, normed_rows = together(
        early, late, gate_grads, y_rows, attended_rows, normed_rows
    )
    late = grid.reduce_axis(late, "u", "u")
    x_rows = grid.from_line(normed_rows, "x")
    grad_probs = grid.reduce_scatter(gate_grads, "yx", "yx").T
    early, late, grad_probs, x_rows = together(early, late, grad_probs, x_rows)
    back_sum, block_out, acc_gate, acc_up, acc_down = together(
        jnp.concatenate([early, late], axis=0), block_out, acc_gate, acc_up, acc_down
    )

    upstream = grad_out.astype(wide)
    grad_logits = router_probs * (
        grad_probs - jnp.sum(router_probs * grad_probs, axis=-1, keepdims=True)
    )
    grad_ffn_normed = back_sum.astype(wide) + jnp.dot(
        grad_logits, router_full.astype(wide).T, precision=lax.Precision.HIGHEST
    )
    grad_router_local = jnp.dot(
        normed_ffn.astype(wide).T, grad_logits, precision=lax.Precision.HIGHEST
    )
    grad_ffn_gain = jnp.sum(grad_ffn_normed * unit_ffn, axis=0)
    grad_mixed = upstream + rms_back(grad_ffn_normed, unit_ffn, ffn_gain, scale_ffn)
    grad_branch = grad_mixed.astype(low)

    output_columns = grid.columns_from_line(grad_branch, "x")
    grad_attended = jnp.einsum(
        "te,de->td", grad_branch, output_full, preferred_element_type=wide
    ).astype(low)
    grad_heads = grad_attended.reshape(tokens_dev, HEADS, HEAD_DIM)
    grad_value_rows = (
        jnp.einsum("hqk,qhd->khd", probs_low, grad_heads, preferred_element_type=wide)
        .reshape(tokens_dev, model_width)
        .astype(low)
    )
    value_columns = grid.columns_from_line(grad_value_rows, "y")
    grad_probs_att = jnp.einsum(
        "qhd,khd->hqk", grad_heads, value_heads, preferred_element_type=wide
    )
    grad_scores = (
        att_probs * (grad_probs_att - jnp.sum(att_probs * grad_probs_att, axis=-1, keepdims=True))
    ).astype(low)
    grad_qrot = (
        jnp.einsum("hqk,khd->qhd", grad_scores, key_rot, preferred_element_type=wide) * inv_root
    )
    grad_krot = (
        jnp.einsum("hqk,qhd->khd", grad_scores, query_rot, preferred_element_type=wide) * inv_root
    )
    grad_qnorm = unrotate(bounce(grad_qrot), cosines, sines).reshape(tokens_dev, model_width)
    grad_knorm = unrotate(bounce(grad_krot), cosines, sines).reshape(tokens_dev, model_width)
    grad_query_gain = jnp.sum(grad_qnorm * unit_query, axis=0)
    grad_key_gain = jnp.sum(grad_knorm * unit_key, axis=0)
    grad_query_raw = rms_back(grad_qnorm, unit_query, query_gain, scale_query).astype(low)
    grad_key_raw = rms_back(grad_knorm, unit_key, key_gain, scale_key).astype(low)
    output_columns, value_columns, grad_query_raw, grad_key_raw = together(
        output_columns, value_columns, grad_query_raw, grad_key_raw
    )

    def outer(left, right):
        total = jnp.einsum("tc,te->ce", left, right, preferred_element_type=wide)
        return total.astype(low).reshape(chips + (weight_rows, -1))

    first = [
        outer(jnp.concatenate(attended_rows, axis=0), output_columns),
        outer(jnp.concatenate(y_rows, axis=0), value_columns),
    ]
    second = [
        grid.columns_from_line(grad_query_raw, "x"),
        grid.columns_from_line(grad_key_raw, "y"),
    ]
    grads = jnp.concatenate([grad_query_raw, grad_key_raw, grad_value_rows], axis=1)
    first, second, grads = together(first, second, grads)
    first = grid.alike(grid.reduce_first(first))
    second = [
        outer(jnp.concatenate(x_rows, axis=0), second[0]),
        outer(jnp.concatenate(y_rows, axis=0), second[1]),
    ]
    grad_attn_normed = turned_product(grads, projections)
    first, second, grad_attn_normed = together(first, second, grad_attn_normed)
    grad_attn_gain = jnp.sum(grad_attn_normed * unit_attn, axis=0)
    grad_input = grad_mixed + rms_back(grad_attn_normed, unit_attn, attn_gain, scale_attn)
    gain_sums = jnp.stack(
        [grad_attn_gain, grad_ffn_gain, grad_query_gain, grad_key_gain], axis=1
    )
    small_sums = jnp.concatenate([grad_router_local, gain_sums], axis=1).reshape(
        grid.shape + (weight_rows, expert_count + gain_sums.shape[1])
    )
    first = grid.reduce_both(first, "w")
    second = grid.alike(grid.reduce_first(second))
    small_sums = grid.reduce_scatter(small_sums, "c")
    first, second, small_sums = together(first, second, small_sums)
    first = grid.reduce_both(first, "u")
    second = grid.reduce_both(second, "w")
    small_sums = grid.reduce_scatter(small_sums, "y", "yxuw")
    first, second, small_sums = together(first, second, small_sums)
    grad_output, grad_value = grid.rows_of_both(first)
    second = grid.reduce_both(second, "u")
    small_sums = grid.reduce_scatter(small_sums, "x", "xuw")
    grad_output, grad_value, second, small_sums = together(
        grad_output, grad_value, second, small_sums
    )
    grad_query, grad_key = grid.rows_of_both(second)
    small_sums = small_sums.reshape((-1,) + small_sums.shape[2:])
    small_sums = grid.reduce_axis(small_sums, "z", "z")
    return (
        block_out,
        grad_input,
        grad_query,
        grad_key,
        grad_value,
        grad_output,
        small_sums[:, :expert_count],
        *(small_sums[:, expert_count + i] for i in range(4)),
        acc_gate,
        acc_up,
        acc_down,
    )


def solution(mesh):
    placed = (
        P(("ep", "tp"), None),
        P(("ep", "tp"), None),
        P(("ep", "tp"), None),
        P(("ep", "tp"), None),
        P(("ep", "tp"), None),
        P(("ep", "tp"), None),
        P(("ep", "tp")),
        P(("ep", "tp")),
        P(("ep", "tp")),
        P(("ep", "tp")),
        P("ep", None, "tp"),
        P("ep", None, "tp"),
        P("ep", "tp", None),
        P(("ep", "tp"), None),
        P(("ep", "tp"), None),
    )
    return jax.shard_map(
        on_device,
        mesh=mesh,
        in_specs=placed,
        out_specs=(
            P(("ep", "tp"), None),
            P(("ep", "tp"), None),
            P(("ep", "tp"), None),
            P(("ep", "tp"), None),
            P(("ep", "tp"), None),
            P(("ep", "tp"), None),
            P(("ep", "tp"), None),
            P(("ep", "tp")),
            P(("ep", "tp")),
            P(("ep", "tp")),
            P(("ep", "tp")),
            P("ep", None, "tp"),
            P("ep", None, "tp"),
            P("ep", "tp", None),
        ),
        check_vma=False,
    )
```

```python
import functools
import math

import jax
import jax.numpy as jnp
from jax import lax
from jax.experimental import pallas as pl
from jax.experimental.pallas import tpu as pltpu
from jax.sharding import PartitionSpec as P

HEADS = 16
HEAD_DIM = 128
CAP = 32


epsilon = 1e-05
rope_base = 10000.0
masked_value = -1e30
low = jnp.bfloat16
wide = jnp.float32


def rope_tables(length, head_dim):
    half_dim = head_dim // 2
    position = jnp.arange(length, dtype=jnp.float32)
    frequency = jnp.exp(
        jnp.arange(half_dim, dtype=jnp.float32) * (-2.0 * math.log(rope_base) / head_dim)
    )
    angles = position[:, None] * frequency[None, :]
    return (jnp.cos(angles)[:, None, :], jnp.sin(angles)[:, None, :])


def rotate(values, cosines, sines):
    half_dim = values.shape[-1] // 2
    first_half = values[..., :half_dim]
    second = values[..., half_dim:]
    return jnp.concatenate(
        [first_half * cosines - second * sines, second * cosines + first_half * sines], axis=-1
    )


def unrotate(grad_vals, cosines, sines):
    half_dim = grad_vals.shape[-1] // 2
    first_half = grad_vals[..., :half_dim]
    second = grad_vals[..., half_dim:]
    return jnp.concatenate(
        [first_half * cosines + second * sines, second * cosines - first_half * sines], axis=-1
    )


def rms_back(grad_normed, unit_vals, gain_vals, inv_scale):
    scaled = grad_normed * gain_vals
    return inv_scale * (scaled - unit_vals * jnp.mean(scaled * unit_vals, axis=-1, keepdims=True))


def bounce(values):
    return lax.optimization_barrier(values.astype(low)).astype(wide)


def after(values, *needs):
    return lax.optimization_barrier((values, needs))[0]


def together(*values):
    return lax.optimization_barrier(values)


def chosen(index, cases):
    return lax.select_n(index.astype(jnp.int32), *cases)


class Grid:
    axes = "yxcuw"

    def __init__(self):
        self.ep, self.tp = lax.axis_size("ep"), lax.axis_size("tp")
        chips = self.ep // 2
        nx = math.isqrt(chips)
        while chips % nx:
            nx -= 1
        nw = 2 - self.tp % 2
        self.size = {"y": chips // nx, "x": nx, "c": 2, "u": self.tp // nw, "w": nw, "z": self.tp}
        self.stride = {"y": 2 * nx, "x": 2, "c": 1, "u": nw, "w": 1, "z": 1}
        self.shape = tuple(self.size[axis] for axis in self.axes)

    def place(self, axis):
        whole = lax.axis_index("tp" if axis in "uwz" else "ep")
        return whole // self.stride[axis] % self.size[axis]

    def shift(self, values, axis, step):
        count, stride = self.size[axis], self.stride[axis]
        pairs = []
        for i in range(self.tp if axis in "uwz" else self.ep):
            own = i // stride % count
            pairs.append((i, i + ((own + step) % count - own) * stride))
        return lax.ppermute(values, "tp" if axis in "uwz" else "ep", pairs)

    def gather_axis(self, values, axis):
        dim, count, own = self.axes.index(axis), self.size[axis], self.place(axis)
        parts = [values] + [self.shift(values, axis, step) for step in range(1, count)]
        shape = list(values.shape)
        shape[dim] = count
        values = jnp.zeros(shape, values.dtype)
        for step, part in enumerate(parts):
            values = lax.dynamic_update_slice_in_dim(values, part, (own - step) % count, dim)
        return values

    def gather(self, values, order):
        values = values[(None,) * len(self.axes)]
        for axis in order:
            values = self.gather_axis(values, axis)
        return values

    def gather_first(self, values):
        rows = values.shape[0]
        values = self.gather(values, "uw")
        halves = values[..., : rows // 2, :], values[..., rows // 2 :, :]
        return [self.gather_axis(half, axis) for half, axis in zip(halves, "xy", strict=True)]

    def gather_second(self, halves):
        halves = [self.gather_axis(half, axis) for half, axis in zip(halves, "yx", strict=True)]
        values = self.gather_axis(jnp.concatenate(halves, axis=-2), "c")
        return values.reshape(-1, values.shape[-1])

    def cut(self, values, axis, axes, steps):
        dim, count, own = axes.index(axis), self.size[axis], self.place(axis)
        return [
            sum(
                lax.dynamic_index_in_dim(v, (own - step) % count, dim, keepdims=False).astype(wide)
                for v in values
            )
            for step in steps
        ]

    def reduce_axis(self, values, axis, axes, cuts=None):
        values = list(values) if isinstance(values, (list, tuple)) else [values]
        kind = values[0].dtype
        if cuts is None:
            cuts = self.cut(values, axis, axes, range(1, self.size[axis]))
        got = [self.shift(cut.astype(kind), axis, -1 - i) for i, cut in enumerate(cuts)]
        if len(values) > 1:
            values = after(tuple(values), *got)
        (total,) = self.cut(values, axis, axes, [0])
        for part in got:
            total = total + part.astype(wide)
        return total.astype(kind)

    def reduce_scatter(self, values, order, axes=axes):
        for axis in order:
            values = self.reduce_axis(values, axis, axes)
            axes = axes.replace(axis, "")
        return values

    def from_line(self, values, axis):
        return [values] + [
            self.shift(values, axis, step) for step in range(1, self.size[axis])
        ]

    def columns_from_line(self, values, axis):
        count, own = self.size[axis], self.place(axis)
        parts = jnp.split(values, count, axis=1)
        taken = [chosen(own, parts)]
        for step in range(1, count):
            taken.append(self.shift(chosen((own + step) % count, parts), axis, step))
        taken = jnp.stack(taken)
        taken = jnp.stack([taken, self.shift(taken, "c", 1)], axis=1)
        return taken.reshape(-1, taken.shape[-1])

    def rows_from_line(self, values, axis):
        count, own = self.size[axis], self.place(axis)
        got = [chosen(own, list(values))]
        for step in range(1, count):
            got.append(self.shift(chosen((own + step) % count, list(values)), axis, step))
        return jnp.concatenate(
            [chosen((own - j) % count, got) for j in range(count)], axis=1
        ).astype(wide)

    def first_cuts(self, pair):
        return [
            [
                cut.astype(low)
                for cut in self.cut(v, axis, "yxuw", range(1, self.size[axis]))
            ]
            for v, axis in zip(pair, "yx", strict=True)
        ]

    def reduce_first(self, pair, cuts=(None, None)):
        return [
            self.reduce_axis(v, axis, "yxuw", cut)
            for v, axis, cut in zip(pair, "yx", cuts, strict=True)
        ]

    def reduce_z(self, pair, turn, lines=("", "")):
        return [
            self.reduce_axis(v, axes[turn], line + (axes[1] if turn else "uw"))
            for v, axes, line in zip(pair, ("wu", "uw"), lines, strict=True)
        ]

    def rows_of_both(self, pair):
        return [self.rows_from_line(v, line) for v, line in zip(pair, "xy", strict=True)]

    def reduce_second(self, pair, join):
        pair = [
            self.reduce_axis(v, axis, axis + "uw") for v, axis in zip(pair, "xy", strict=True)
        ]
        return pair if join is None else jnp.concatenate(pair, axis=join + 2)

    def chips(self):
        return tuple(self.size[axis] for axis in "yxuw")


nt_dims = (((1,), (1,)), ((), ()))
tn_dims = (((0,), (0,)), ((), ()))


def one_hot(slots):
    experts, tokens = slots.shape
    place = lax.broadcasted_iota(jnp.int32, (experts, CAP, tokens), 1).astype(wide) + 1.0
    return (slots[:, None, :] == place).astype(wide).reshape(experts * CAP, tokens)


def dot(left, right, dims=(((1,), (0,)), ((), ()))):
    return lax.dot_general(left, right, dims, preferred_element_type=wide)


def gate_column(pick, gates):
    spread = jnp.broadcast_to(gates[:, None, :], (gates.shape[0], CAP, gates.shape[1]))
    return jnp.sum(pick * spread.reshape(pick.shape), axis=1, keepdims=True)


def product_kernel(left_ref, right_ref, out_ref):
    out_ref[...] = dot(left_ref[...], right_ref[...], nt_dims)


def turned_product(left, right, block=256):
    rows, depth = left.shape
    columns = right.shape[0]
    return pl.pallas_call(
        product_kernel,
        grid=(columns // block,),
        in_specs=[
            pl.BlockSpec((rows, depth), lambda i: (0, 0)),
            pl.BlockSpec((block, depth), lambda i: (i, 0)),
        ],
        out_specs=pl.BlockSpec((rows, block), lambda i: (0, i)),
        out_shape=jax.ShapeDtypeStruct((rows, columns), wide),
        compiler_params=pltpu.CompilerParams(vmem_limit_bytes=40 * 1024 * 1024),
        cost_estimate=pl.CostEstimate(
            flops=50 * rows * depth * columns, bytes_accessed=columns * depth * 2, transcendentals=0
        ),
        name="turned_product",
    )(left, right)


class Streams:
    def __init__(self, sources, targets, sems, rows_v, rows_hbm, row_sem, base):
        self.step, chunk = pl.program_id(0), rows_v.shape[0]
        experts = sources[0].shape[0]
        self.groups = [range(experts // 2), range(experts // 2, experts)]
        self.weights = [
            [
                pltpu.make_async_copy(source.at[e], target(e), sems.at[i, e])
                for i, (source, target) in enumerate(zip(sources, targets, strict=True))
                for e in group
            ]
            for group in self.groups
        ]
        block = base + self.step * chunk
        self.rows = [
            pltpu.make_async_copy(
                rows_v.at[:, e * CAP : (e + 1) * CAP, :],
                rows_hbm.at[e, pl.ds(block, chunk)],
                row_sem.at[e],
            )
            for e in range(experts)
        ]

        @pl.when(self.step == 0)
        def _():
            for copies in self.weights:
                for copy in copies:
                    copy.start()

        @pl.when(self.step > 0)
        def _():
            self.wait_rows()

    def wait_rows(self):
        for copy in self.rows:
            copy.wait()

    def send_rows(self):
        for copy in self.rows:
            copy.start()

    def wait_weights(self, group):
        @pl.when(self.step == 0)
        def _():
            for copy in self.weights[group]:
                copy.wait()

    def end(self):
        @pl.when(self.step == pl.num_programs(0) - 1)
        def _():
            self.wait_rows()


def write_parts(targets, block, total):
    share = total.shape[0] // len(targets)
    for i, target in enumerate(targets):
        target[block] = total[i * share : (i + 1) * share]


def forward_kernel(base, kept, parts, _, slots_ref, router_ref, x_ref, *refs):
    weights, refs = refs[:3], refs[3:]
    refs = refs[kept:]
    y_refs, refs = refs[:parts], refs[parts:]
    gates_ref, pre_ref, inner_ref, rows_hbm = refs[:4]
    joint_w, down_w, rows_v, out_v, gate_rows, w_sems, row_sems = refs[4:]
    chunk, _, width = x_ref.shape
    experts, hidden, _ = down_w.shape
    depth = chunk * CAP
    targets = (
        lambda e: joint_w.at[e, :, :hidden],
        lambda e: joint_w.at[e, :, hidden:],
        lambda e: down_w.at[e],
    )
    streams = Streams(weights, targets, w_sems, rows_v, rows_hbm, row_sems, base)
    picks = []
    for b in range(chunk):
        tokens = x_ref[b]
        logits = dot(tokens, router_ref[...]).T
        exponent = jnp.exp(logits - jnp.max(logits, axis=0, keepdims=True))
        gates = (exponent / jnp.sum(exponent, axis=0, keepdims=True))[:experts]
        gates_ref[b] = gates
        pick = one_hot(slots_ref[b])
        gate_rows[b] = gate_column(pick, gates)
        picks.append(pick.astype(low))
        rows_v[b] = dot(picks[b], tokens).astype(low)
    streams.send_rows()
    for e in range(experts):
        at = slice(e * CAP, (e + 1) * CAP)
        for i, group in enumerate(streams.groups):
            if e == group.start:
                streams.wait_weights(i)
        pre = dot(rows_v[:, at, :].reshape(depth, width), joint_w[e])
        pre_ref[e] = pre
        gate_pre, up_pre = pre[:, :hidden], pre[:, hidden:]
        inner = (gate_pre * jax.nn.sigmoid(gate_pre) * up_pre).astype(low).astype(wide)
        scaled = (inner * gate_rows[:, at, :].reshape(depth, 1)).astype(low)
        inner_ref[e] = scaled
        out = dot(scaled, down_w[e]).astype(low)
        out_v[:, at, :] = out.reshape(chunk, CAP, width)
    for b in range(chunk):
        write_parts(y_refs, b, dot(picks[b], out_v[b], tn_dims).astype(low))
    streams.end()


def backward_kernel(base, kept, parts, _, slots_ref, gates_ref, g_ref, pre_ref, *refs):
    weights, refs = refs[:3], refs[3:]
    refs = refs[kept:]
    x_refs, refs = refs[:parts], refs[parts:]
    grads_ref, dgate_ref, dup_ref, rows_hbm = refs[:4]
    joint_w, down_w, rows_v, out_v, gate_rows, grad_rows, w_sems, row_sems = refs[4:]
    chunk, _, width = g_ref.shape
    tokens = slots_ref.shape[2]
    experts, _, hidden = down_w.shape
    depth = chunk * CAP
    targets = (
        lambda e: joint_w.at[e, :hidden],
        lambda e: joint_w.at[e, hidden:],
        lambda e: down_w.at[e],
    )
    streams = Streams(weights, targets, w_sems, rows_v, rows_hbm, row_sems, base)
    picks = []
    for b in range(chunk):
        pick = one_hot(slots_ref[b])
        gate_rows[b] = gate_column(pick, gates_ref[b])
        picks.append(pick.astype(low))
        rows_v[b] = dot(picks[b], g_ref[b]).astype(low)
    streams.send_rows()
    for e in range(experts):
        at = slice(e * CAP, (e + 1) * CAP)
        for i, group in enumerate(streams.groups):
            if e == group.start:
                streams.wait_weights(i)
        pulled = dot(rows_v[:, at, :].reshape(depth, width), down_w[e])
        gate_pre, up_pre = pre_ref[e, :, :hidden], pre_ref[e, :, hidden:]
        sigmoid = jax.nn.sigmoid(gate_pre)
        silu = gate_pre * sigmoid
        inner = (silu * up_pre).astype(low).astype(wide)
        grad_rows[:, at, :] = jnp.sum(inner * pulled, axis=1, keepdims=True).reshape(
            chunk, CAP, 1
        )
        grad_inner = pulled * gate_rows[:, at, :].reshape(depth, 1)
        dgate = (grad_inner * up_pre * sigmoid * (1.0 + gate_pre * (1.0 - sigmoid))).astype(low)
        dup = (grad_inner * silu).astype(low)
        dgate_ref[e] = dgate
        dup_ref[e] = dup
        out = dot(jnp.concatenate([dgate, dup], axis=1), joint_w[e]).astype(low)
        out_v[:, at, :] = out.reshape(chunk, CAP, width)
    for b in range(chunk):
        write_parts(x_refs, b, dot(picks[b], out_v[b], tn_dims).astype(low))
        per_row = picks[b].astype(wide) * grad_rows[b]
        grads_ref[b] = jnp.sum(per_row.reshape(experts, CAP, tokens), axis=1)
    streams.end()


class Experts:
    def __init__(self, blocks, chunk, tokens, width, experts, hidden):
        self.chunk, self.half = chunk, blocks // 2
        self.tokens, self.width, self.experts, self.hidden = tokens, width, experts, hidden
        self.rows = blocks * CAP

    def mine(self, first, *shape):
        return pl.BlockSpec(
            (self.chunk,) + shape,
            lambda i, core: (2 * (i + first) + core[0],) + (0,) * len(shape),
        )

    def listed(self, first, *shape):
        return pl.BlockSpec(
            (self.chunk,) + shape, lambda i, core: (i + first,) + (0,) * len(shape)
        )

    def by_row(self, last, first):
        return pl.BlockSpec(
            (self.experts, self.chunk * CAP, last), lambda i, core: (0, i + first, 0)
        )

    def call(self, kernel, name, first, count, turn, parts, core, ins, in_specs, outs, given):
        any_spec = pl.BlockSpec(memory_space=pl.ANY)
        base = turn * self.half + first * self.chunk
        joint = [self.experts, self.width, self.width]
        joint[2 if kernel is forward_kernel else 1] = 2 * self.hidden
        given = [None] * (len(outs) - len(given)) + given
        goes_on = [i for i, array in enumerate(given) if array is not None]
        rows = self.experts * count * self.chunk * CAP
        results = pl.pallas_call(
            functools.partial(kernel, base, len(goes_on), parts),
            grid_spec=pltpu.PrefetchScalarGridSpec(
                num_scalar_prefetch=1,
                grid=(count,),
                in_specs=in_specs + [any_spec] * (3 + len(goes_on)),
                out_specs=[spec or any_spec for _, _, spec in outs],
                scratch_shapes=[pltpu.VMEM(tuple(joint), low), pltpu.VMEM(ins[-1].shape, low)]
                + [pltpu.VMEM((self.chunk, self.experts * CAP, self.width), low)] * 2
                + [pltpu.VMEM((self.chunk, self.experts * CAP, 1), wide)] * (1 if kernel is forward_kernel else 2)
                + [
                    pltpu.SemaphoreType.DMA((3, self.experts)),
                    pltpu.SemaphoreType.DMA((self.experts,)),
                ],
            ),
            out_shape=[jax.ShapeDtypeStruct(shape, kind) for shape, kind, _ in outs],
            input_output_aliases={1 + len(ins) + n: i for n, i in enumerate(goes_on)},
            compiler_params=pltpu.CompilerParams(
                dimension_semantics=("arbitrary",), vmem_limit_bytes=60 * 1024 * 1024
            ),
            cost_estimate=pl.CostEstimate(
                flops=10 * rows * self.width * (3 * self.hidden + 256),
                bytes_accessed=rows * self.width * 8,
                transcendentals=0,
            ),
            name=name,
        )(core, *ins, *(given[i] for i in goes_on))
        return list(results)

    def token_outs(self, first, parts):
        share = self.tokens // parts
        part = ((self.half, share, self.width), low, self.listed(first, share, self.width))
        by_token = (
            (self.half, self.experts, self.tokens),
            wide,
            self.listed(first, self.experts, self.tokens),
        )
        return [part] * parts + [by_token]

    def row_out(self, first, turn):
        first += turn * self.half // self.chunk
        return (
            (self.experts, self.rows, self.hidden),
            low,
            self.by_row(self.hidden, first),
        )

    def taken(self):
        return ((self.experts, self.rows // CAP, CAP, self.width), low, None)

    def forward(self, first, count, turn, parts, core, slots, router, tokens, weights, given):
        pre = (
            (self.experts, self.half * CAP, 2 * self.hidden),
            wide,
            self.by_row(2 * self.hidden, first),
        )
        return self.call(
            forward_kernel,
            "experts_forward",
            first,
            count,
            turn,
            parts,
            core,
            (slots, router, tokens, *weights),
            [
                self.mine(first, self.experts, self.tokens),
                pl.BlockSpec(router.shape, lambda i, core: (0, 0)),
                self.mine(first, self.tokens, self.width),
            ],
            self.token_outs(first, parts) + [pre, self.row_out(first, turn), self.taken()],
            given,
        )

    def backward(
        self, first, count, turn, parts, core, slots, gates, grads, pre, weights, given
    ):
        return self.call(
            backward_kernel,
            "experts_backward",
            first,
            count,
            turn,
            parts,
            core,
            (slots, gates, grads, pre, *weights),
            [
                self.mine(first, self.experts, self.tokens),
                self.listed(first, self.experts, self.tokens),
                self.mine(first, self.tokens, self.width),
                self.by_row(2 * self.hidden, first),
            ],
            self.token_outs(first, parts)
            + [self.row_out(first, turn), self.row_out(first, turn), self.taken()],
            given,
        )


def on_device(
    hidden_in,
    w_query,
    w_key,
    w_value,
    w_output,
    w_router,
    gain_attn,
    gain_ffn,
    gain_query,
    gain_key,
    w_gate,
    w_up,
    w_down,
    expert_ids,
    grad_out,
):
    tokens_dev, model_width = hidden_in.shape
    local_experts, _, hidden_units = w_gate.shape
    expert_count = w_router.shape[1]
    grid = Grid()
    blocks = grid.ep * grid.tp
    weight_rows = model_width // blocks
    both = ("ep", "tp")
    inv_root = 1.0 / math.sqrt(HEAD_DIM)

    def gathered(values):
        return lax.all_gather(values, both, axis=0, tiled=True)

    named = jnp.any(
        expert_ids[None, :, :] == jnp.arange(expert_count, dtype=jnp.int32)[:, None, None], axis=2
    )
    before = (jnp.arange(tokens_dev)[:, None] <= jnp.arange(tokens_dev)[None, :]).astype(low)
    counted = jnp.dot(named.astype(low), before, preferred_element_type=wide)
    slots = jnp.where(named, counted, 0.0).astype(low)

    shared = jnp.concatenate(
        [
            w_router,
            jnp.stack([gain_attn, gain_ffn, gain_query, gain_key], axis=1),
            jnp.zeros((w_router.shape[0], tokens_dev - expert_count - 4), low),
        ],
        axis=1,
    )
    output_full = grid.gather_second(grid.gather_first(w_output))
    small_all = after(jnp.concatenate([shared, slots], axis=0), output_full)
    small_all = grid.gather(small_all, "xyuwc")
    small_all = small_all.reshape(blocks, weight_rows + expert_count, tokens_dev)
    shared_full = small_all[:, :weight_rows].reshape(model_width, tokens_dev)
    slots_all = small_all[:, weight_rows:]
    router_full = shared_full[:, :expert_count]
    gains = shared_full[:, expert_count : expert_count + 4].astype(wide).T
    attn_gain, ffn_gain, query_gain, key_gain = gains[0], gains[1], gains[2], gains[3]

    projections = gathered(jnp.concatenate([w_query, w_key, w_value], axis=1))
    inputs_full = hidden_in.astype(wide)
    scale_attn = lax.rsqrt(jnp.mean(inputs_full * inputs_full, axis=-1, keepdims=True) + epsilon)
    unit_attn = inputs_full * scale_attn
    normed_attn = (unit_attn * attn_gain).astype(low)
    projections, output_full, normed_attn, query_gain, key_gain, ffn_gain = together(
        projections,
        output_full,
        normed_attn,
        query_gain,
        key_gain,
        ffn_gain,
    )
    upstream_all = gathered(after(grad_out, projections)[None])
    projected = jnp.dot(normed_attn, projections, preferred_element_type=wide)
    query_raw = projected[:, :model_width]
    key_raw = projected[:, model_width : 2 * model_width]
    value_raw = projected[:, 2 * model_width :]
    scale_query = lax.rsqrt(jnp.mean(query_raw * query_raw, axis=-1, keepdims=True) + epsilon)
    unit_query = query_raw * scale_query
    scale_key = lax.rsqrt(jnp.mean(key_raw * key_raw, axis=-1, keepdims=True) + epsilon)
    unit_key = key_raw * scale_key
    cosines, sines = rope_tables(tokens_dev, HEAD_DIM)
    query_rot = rotate(
        (unit_query * query_gain).reshape(tokens_dev, HEADS, HEAD_DIM), cosines, sines
    ).astype(low)
    key_rot = rotate(
        (unit_key * key_gain).reshape(tokens_dev, HEADS, HEAD_DIM), cosines, sines
    ).astype(low)
    value_heads = value_raw.astype(low).reshape(tokens_dev, HEADS, HEAD_DIM)
    causal = jnp.arange(tokens_dev)[:, None] >= jnp.arange(tokens_dev)[None, :]
    scores = (
        jnp.einsum("qhd,khd->hqk", query_rot, key_rot, preferred_element_type=wide) * inv_root
    )
    scores = jnp.where(causal[None], scores, masked_value)
    exponent = jnp.exp(scores - jnp.max(scores, axis=-1, keepdims=True))
    att_probs = exponent / jnp.sum(exponent, axis=-1, keepdims=True)
    probs_low = att_probs.astype(low)
    attended = (
        jnp.einsum("hqk,khd->qhd", probs_low, value_heads, preferred_element_type=wide)
        .reshape(tokens_dev, model_width)
        .astype(low)
    )
    mixed = inputs_full + jnp.dot(attended, output_full, preferred_element_type=wide)
    scale_ffn = lax.rsqrt(jnp.mean(mixed * mixed, axis=-1, keepdims=True) + epsilon)
    unit_ffn = mixed * scale_ffn
    normed_ffn = (unit_ffn * ffn_gain).astype(low)
    normed_all = gathered(normed_ffn[None])
    router_probs = jax.nn.softmax(
        jnp.dot(normed_ffn, router_full, preferred_element_type=wide), axis=-1
    )

    turned = [weights.transpose(0, 2, 1) for weights in (w_gate, w_up, w_down)]
    normed_all, turned = together(normed_all, turned)

    first_expert = lax.axis_index("ep") * local_experts
    slots_here = lax.dynamic_slice_in_dim(slots_all, first_expert, local_experts, 1).astype(wide)
    router_turned = lax.dynamic_slice_in_dim(
        jnp.concatenate([router_full, router_full], axis=1), first_expert, expert_count, 1
    )
    experts = Experts(
        blocks, grid.tp, tokens_dev, model_width, local_experts, hidden_units
    )
    core = grid.place("c")
    turns = (jnp.reshape(1 - core, (1,)), jnp.reshape(core, (1,)))
    chips = grid.chips()

    def token_sums(away, kept):
        return [
            [half.reshape(chips + half.shape[1:]) for half in pair]
            for pair in zip(away, kept, strict=True)
        ]

    groups = blocks // 2 // grid.tp
    forward_ins = (slots_here, router_turned, normed_all, (w_gate, w_up, w_down))
    *y_ahead, gates_ahead, pre_ahead, inner_scaled, rows_in = experts.forward(
        0, groups, 0, 2, turns[0], *forward_ins, []
    )
    *y_own, gates_own, pre_own, inner_scaled, rows_in = experts.forward(
        0, groups, 1, 2, turns[1], *forward_ins, [inner_scaled, rows_in]
    )
    y_away = [grid.shift(half, "c", 1) for half in y_ahead]
    y_own, y_away, gates_own, slots_here = together(y_own, y_away, gates_own, slots_here)
    expert_sums = token_sums(y_away, y_own)
    cuts = grid.first_cuts(expert_sums)
    cuts, upstream_all, slots_here = together(cuts, upstream_all, slots_here)

    def backward(first, count, turn, parts, gates, pre, given):
        return experts.backward(
            first,
            count,
            turn,
            parts,
            turns[turn],
            slots_here,
            gates,
            upstream_all,
            pre,
            turned,
            given,
        )

    def by_core(values):
        parts = jnp.split(values, 2 * chips[0] * chips[1], axis=1)
        cut = [jnp.concatenate(parts[at::2], axis=1) for at in range(2)]
        return [chosen(at, cut) for at in (1 - core, core)]

    away, kept = (
        jnp.concatenate(cut, axis=1)
        for cut in zip(by_core(normed_attn), by_core(attended), strict=True)
    )
    ahead = backward(0, groups, 0, 2, gates_ahead, pre_ahead, [])
    expert_sums = grid.reduce_first(expert_sums, cuts)
    pair_rows = [kept, grid.shift(away, "c", 1)]
    (*x_ahead, gate_grads_ahead, dgate, dup, taken), expert_sums, slots_here, pair_rows = together(
        ahead, expert_sums, slots_here, pair_rows
    )
    x_away = [grid.shift(half, "c", 1) for half in x_ahead]
    own = backward(0, groups, 1, 2, gates_own, pre_own, [dgate, dup, taken])
    expert_sum = grid.reduce_second(expert_sums, 0)
    own, expert_sum, x_away = together(own, expert_sum, x_away)
    *x_own, gate_grads_own, grad_gate_part, grad_up_part, rows_up = own
    rows_in = rows_in.reshape(local_experts, -1, model_width)
    rows_up = rows_up.reshape(local_experts, -1, model_width)

    def weight_grad(subscripts, left, right):
        return jnp.einsum(subscripts, left, right, preferred_element_type=wide)

    sums = token_sums(x_away, x_own)
    gate_grads = jnp.stack([gate_grads_own, gate_grads_ahead])
    gate_grads = jnp.where(core == 0, gate_grads, gate_grads[::-1])
    gate_grads = gate_grads.reshape((2,) + chips + (local_experts, tokens_dev))
    acc_gate = weight_grad("erd,erh->edh", rows_in, grad_gate_part)
    acc_down = weight_grad("erh,erd->ehd", inner_scaled, rows_up)
    sums = grid.reduce_first(sums)
    expert_sum = grid.reduce_axis(expert_sum, "w", "uw")
    gate_grads = grid.reduce_axis(gate_grads, "w", "cyxuw")
    sums, acc_gate, acc_down, expert_sum, rows_in, gate_grads = together(
        sums, acc_gate, acc_down, expert_sum, rows_in, gate_grads
    )
    acc_up = weight_grad("erd,erh->edh", rows_in, grad_up_part)
    sums = grid.reduce_second(sums, None)
    expert_sum = grid.reduce_axis(expert_sum, "u", "u")
    gate_grads = grid.reduce_axis(gate_grads, "u", "cyxu")
    gate_grads = lax.dynamic_update_slice_in_dim(
        jnp.zeros(gate_grads.shape[:3] + (expert_count, tokens_dev), wide),
        gate_grads,
        first_expert,
        3,
    )
    sums, acc_up, expert_sum, gate_grads, pair_rows = together(
        sums, acc_up, expert_sum, gate_grads, pair_rows
    )
    block_out = (mixed + expert_sum.astype(wide)).astype(low)
    sums = grid.reduce_z(sums, 0)
    gate_grads = grid.reduce_axis(gate_grads, "c", "cyx")
    pair_rows = jnp.concatenate(pair_rows, axis=0)
    half = model_width // 2
    y_rows = grid.from_line(pair_rows[:, :half], "y")
    x_rows = grid.from_line(pair_rows, "x")
    sums, gate_grads, y_rows, x_rows = together(sums, gate_grads, y_rows, x_rows)
    back_sum = jnp.concatenate(grid.reduce_z(sums, 1), axis=0)
    grad_probs = grid.reduce_scatter(gate_grads, "yx", "yx").T
    back_sum, grad_probs = together(back_sum, grad_probs)
    y_rows, x_rows = jnp.concatenate(y_rows, axis=0), jnp.concatenate(x_rows, axis=0)
    back_sum, block_out, acc_gate, acc_up, acc_down = together(
        back_sum, block_out, acc_gate, acc_up, acc_down
    )

    upstream = grad_out.astype(wide)
    grad_logits = router_probs * (
        grad_probs - jnp.sum(router_probs * grad_probs, axis=-1, keepdims=True)
    )
    grad_ffn_normed = back_sum.astype(wide) + jnp.dot(
        grad_logits, router_full.astype(wide).T, precision=lax.Precision.HIGHEST
    )
    grad_ffn_gain = jnp.sum(grad_ffn_normed * unit_ffn, axis=0)
    grad_mixed = upstream + rms_back(grad_ffn_normed, unit_ffn, ffn_gain, scale_ffn)
    grad_branch = grad_mixed.astype(low)

    output_columns = grid.columns_from_line(grad_branch, "x")
    grad_attended = jnp.einsum(
        "te,de->td", grad_branch, output_full, preferred_element_type=wide
    ).astype(low)
    grad_heads = grad_attended.reshape(tokens_dev, HEADS, HEAD_DIM)
    grad_value_rows = (
        jnp.einsum("hqk,qhd->khd", probs_low, grad_heads, preferred_element_type=wide)
        .reshape(tokens_dev, model_width)
        .astype(low)
    )
    value_columns = grid.columns_from_line(grad_value_rows, "y")
    grad_probs_att = jnp.einsum(
        "qhd,khd->hqk", grad_heads, value_heads, preferred_element_type=wide
    )
    grad_scores = (
        att_probs * (grad_probs_att - jnp.sum(att_probs * grad_probs_att, axis=-1, keepdims=True))
    ).astype(low)
    grad_qrot = (
        jnp.einsum("hqk,khd->qhd", grad_scores, key_rot, preferred_element_type=wide) * inv_root
    )
    grad_krot = (
        jnp.einsum("hqk,qhd->khd", grad_scores, query_rot, preferred_element_type=wide) * inv_root
    )
    grad_qnorm = unrotate(bounce(grad_qrot), cosines, sines).reshape(tokens_dev, model_width)
    grad_knorm = unrotate(bounce(grad_krot), cosines, sines).reshape(tokens_dev, model_width)
    grad_query_gain = jnp.sum(grad_qnorm * unit_query, axis=0)
    grad_key_gain = jnp.sum(grad_knorm * unit_key, axis=0)
    grad_query_raw = rms_back(grad_qnorm, unit_query, query_gain, scale_query).astype(low)
    grad_key_raw = rms_back(grad_knorm, unit_key, key_gain, scale_key).astype(low)
    output_columns, value_columns, grad_query_raw, grad_key_raw = together(
        output_columns, value_columns, grad_query_raw, grad_key_raw
    )

    def outer(left, right):
        total = jnp.einsum("tc,te->ce", left, right, preferred_element_type=wide)
        return total.astype(low).reshape(chips + (weight_rows, -1))

    first = [
        outer(x_rows[:, half:], output_columns),
        outer(y_rows, value_columns),
    ]
    second = [
        grid.columns_from_line(grad_query_raw, "x"),
        grid.columns_from_line(grad_key_raw, "y"),
    ]
    grads = jnp.concatenate([grad_query_raw, grad_key_raw, grad_value_rows], axis=1)
    first, second, grads = together(first, second, grads)
    first = grid.reduce_first(first)
    second = [
        outer(x_rows[:, :half], second[0]),
        outer(y_rows, second[1]),
    ]
    grad_attn_normed = turned_product(grads, projections)
    first, second, grad_attn_normed, grad_logits = together(
        first, second, grad_attn_normed, grad_logits
    )
    grad_router_local = jnp.dot(
        normed_ffn.astype(wide).T, grad_logits, precision=lax.Precision.HIGHEST
    )
    grad_attn_gain = jnp.sum(grad_attn_normed * unit_attn, axis=0)
    grad_input = grad_mixed + rms_back(grad_attn_normed, unit_attn, attn_gain, scale_attn)
    gain_sums = jnp.stack(
        [grad_attn_gain, grad_ffn_gain, grad_query_gain, grad_key_gain], axis=1
    )
    small_sums = jnp.concatenate([grad_router_local, gain_sums], axis=1).reshape(
        grid.shape + (weight_rows, expert_count + gain_sums.shape[1])
    )
    first = grid.reduce_z(first, 0, "xy")
    second = grid.reduce_first(second)
    first, second, small_sums = together(first, second, small_sums)
    first = grid.reduce_z(first, 1, "xy")
    second = grid.reduce_z(second, 0, "xy")
    small_sums = grid.reduce_scatter(small_sums, "cy")
    first, second, small_sums = together(first, second, small_sums)
    grad_output, grad_value = grid.rows_of_both(first)
    second = grid.reduce_z(second, 1, "xy")
    small_sums = grid.reduce_scatter(small_sums, "x", "xuw")
    grad_output, grad_value, second, small_sums = together(
        grad_output, grad_value, second, small_sums
    )
    grad_query, grad_key = grid.rows_of_both(second)
    small_sums = small_sums.reshape((-1,) + small_sums.shape[2:])
    small_sums = grid.reduce_axis(small_sums, "z", "z")
    return (
        block_out,
        grad_input,
        grad_query,
        grad_key,
        grad_value,
        grad_output,
        small_sums[:, :expert_count],
        *(small_sums[:, expert_count + i] for i in range(4)),
        acc_gate,
        acc_up,
        acc_down,
    )


def solution(mesh):
    placed = (
        P(("ep", "tp"), None),
        P(("ep", "tp"), None),
        P(("ep", "tp"), None),
        P(("ep", "tp"), None),
        P(("ep", "tp"), None),
        P(("ep", "tp"), None),
        P(("ep", "tp")),
        P(("ep", "tp")),
        P(("ep", "tp")),
        P(("ep", "tp")),
        P("ep", None, "tp"),
        P("ep", None, "tp"),
        P("ep", "tp", None),
        P(("ep", "tp"), None),
        P(("ep", "tp"), None),
    )
    return jax.shard_map(
        on_device,
        mesh=mesh,
        in_specs=placed,
        out_specs=(
            P(("ep", "tp"), None),
            P(("ep", "tp"), None),
            P(("ep", "tp"), None),
            P(("ep", "tp"), None),
            P(("ep", "tp"), None),
            P(("ep", "tp"), None),
            P(("ep", "tp"), None),
            P(("ep", "tp")),
            P(("ep", "tp")),
            P(("ep", "tp")),
            P(("ep", "tp")),
            P("ep", None, "tp"),
            P("ep", None, "tp"),
            P("ep", "tp", None),
        ),
        check_vma=False,
    )
```

```python
import functools
import math

import jax
import jax.numpy as jnp
from jax import lax
from jax.experimental import pallas as pl
from jax.experimental.pallas import tpu as pltpu
from jax.sharding import PartitionSpec as P

HEADS = 16
HEAD_DIM = 128
CAP = 32


epsilon = 1e-05
rope_base = 10000.0
masked_value = -1e30
low = jnp.bfloat16
wide = jnp.float32


def rope_tables(length, head_dim):
    half_dim = head_dim // 2
    position = jnp.arange(length, dtype=jnp.float32)
    frequency = jnp.exp(
        jnp.arange(half_dim, dtype=jnp.float32) * (-2.0 * math.log(rope_base) / head_dim)
    )
    angles = position[:, None] * frequency[None, :]
    return (jnp.cos(angles)[:, None, :], jnp.sin(angles)[:, None, :])


def rotate(values, cosines, sines):
    half_dim = values.shape[-1] // 2
    first_half = values[..., :half_dim]
    second = values[..., half_dim:]
    return jnp.concatenate(
        [first_half * cosines - second * sines, second * cosines + first_half * sines], axis=-1
    )


def unrotate(grad_vals, cosines, sines):
    half_dim = grad_vals.shape[-1] // 2
    first_half = grad_vals[..., :half_dim]
    second = grad_vals[..., half_dim:]
    return jnp.concatenate(
        [first_half * cosines + second * sines, second * cosines - first_half * sines], axis=-1
    )


def rms_back(grad_normed, unit_vals, gain_vals, inv_scale):
    scaled = grad_normed * gain_vals
    return inv_scale * (scaled - unit_vals * jnp.mean(scaled * unit_vals, axis=-1, keepdims=True))


def bounce(values):
    return lax.optimization_barrier(values.astype(low)).astype(wide)


def after(values, *needs):
    return lax.optimization_barrier((values, needs))[0]


def together(*values):
    return lax.optimization_barrier(values)


def chosen(index, cases):
    return lax.select_n(index.astype(jnp.int32), *cases)


class Grid:
    axes = "yxcuw"

    def __init__(self):
        self.ep, self.tp = lax.axis_size("ep"), lax.axis_size("tp")
        chips = self.ep // 2
        nx = math.isqrt(chips)
        while chips % nx:
            nx -= 1
        nw = 2 - self.tp % 2
        self.size = {"y": chips // nx, "x": nx, "c": 2, "u": self.tp // nw, "w": nw, "z": self.tp}
        self.stride = {"y": 2 * nx, "x": 2, "c": 1, "u": nw, "w": 1, "z": 1}
        self.shape = tuple(self.size[axis] for axis in self.axes)

    def place(self, axis):
        whole = lax.axis_index("tp" if axis in "uwz" else "ep")
        return whole // self.stride[axis] % self.size[axis]

    def shift(self, values, axis, step):
        count, stride = self.size[axis], self.stride[axis]
        pairs = []
        for i in range(self.tp if axis in "uwz" else self.ep):
            own = i // stride % count
            pairs.append((i, i + ((own + step) % count - own) * stride))
        return lax.ppermute(values, "tp" if axis in "uwz" else "ep", pairs)

    def gather_axis(self, values, axis):
        dim, count, own = self.axes.index(axis), self.size[axis], self.place(axis)
        parts = [values] + [self.shift(values, axis, step) for step in range(1, count)]
        shape = list(values.shape)
        shape[dim] = count
        values = jnp.zeros(shape, values.dtype)
        for step, part in enumerate(parts):
            values = lax.dynamic_update_slice_in_dim(values, part, (own - step) % count, dim)
        return values

    def gather(self, values, order):
        values = values[(None,) * len(self.axes)]
        for axis in order:
            values = self.gather_axis(values, axis)
        return values

    def gather_first(self, values):
        rows = values.shape[0]
        values = self.gather(values, "uw")
        halves = values[..., : rows // 2, :], values[..., rows // 2 :, :]
        return [self.gather_axis(half, axis) for half, axis in zip(halves, "xy", strict=True)]

    def gather_second(self, halves):
        halves = [self.gather_axis(half, axis) for half, axis in zip(halves, "yx", strict=True)]
        values = self.gather_axis(jnp.concatenate(halves, axis=-2), "c")
        return values.reshape(-1, values.shape[-1])

    def cut(self, values, axis, axes, steps):
        dim, count, own = axes.index(axis), self.size[axis], self.place(axis)
        return [
            sum(
                lax.dynamic_index_in_dim(v, (own - step) % count, dim, keepdims=False).astype(wide)
                for v in values
            )
            for step in steps
        ]

    def reduce_axis(self, values, axis, axes, cuts=None):
        values = list(values) if isinstance(values, (list, tuple)) else [values]
        kind = values[0].dtype
        if cuts is None:
            cuts = self.cut(values, axis, axes, range(1, self.size[axis]))
        got = [self.shift(cut.astype(kind), axis, -1 - i) for i, cut in enumerate(cuts)]
        if len(values) > 1:
            values = after(tuple(values), *got)
        (total,) = self.cut(values, axis, axes, [0])
        for part in got:
            total = total + part.astype(wide)
        return total.astype(kind)

    def reduce_scatter(self, values, order, axes=axes):
        for axis in order:
            values = self.reduce_axis(values, axis, axes)
            axes = axes.replace(axis, "")
        return values

    def from_line(self, values, axis):
        return [values] + [
            self.shift(values, axis, step) for step in range(1, self.size[axis])
        ]

    def columns_from_line(self, values, axis):
        count, own = self.size[axis], self.place(axis)
        parts = jnp.split(values, count, axis=1)
        taken = [chosen(own, parts)]
        for step in range(1, count):
            taken.append(self.shift(chosen((own + step) % count, parts), axis, step))
        taken = jnp.stack(taken)
        taken = jnp.stack([taken, self.shift(taken, "c", 1)], axis=1)
        return taken.reshape(-1, taken.shape[-1])

    def rows_from_line(self, values, axis):
        count, own = self.size[axis], self.place(axis)
        got = [chosen(own, list(values))]
        for step in range(1, count):
            got.append(self.shift(chosen((own + step) % count, list(values)), axis, step))
        return jnp.concatenate(
            [chosen((own - j) % count, got) for j in range(count)], axis=1
        ).astype(wide)

    def first_cuts(self, pair):
        return [
            [
                cut.astype(low)
                for cut in self.cut(v, axis, "yxuw", range(1, self.size[axis]))
            ]
            for v, axis in zip(pair, "yx", strict=True)
        ]

    def reduce_first(self, pair, cuts=(None, None)):
        return [
            self.reduce_axis(v, axis, "yxuw", cut)
            for v, axis, cut in zip(pair, "yx", cuts, strict=True)
        ]

    def reduce_z(self, pair, turn, lines=("", "")):
        return [
            self.reduce_axis(v, axes[turn], line + (axes[1] if turn else "uw"))
            for v, axes, line in zip(pair, ("wu", "uw"), lines, strict=True)
        ]

    def rows_of_both(self, pair):
        return [self.rows_from_line(v, line) for v, line in zip(pair, "xy", strict=True)]

    def reduce_second(self, pair, join):
        pair = [
            self.reduce_axis(v, axis, axis + "uw") for v, axis in zip(pair, "xy", strict=True)
        ]
        return pair if join is None else jnp.concatenate(pair, axis=join + 2)

    def chips(self):
        return tuple(self.size[axis] for axis in "yxuw")


nt_dims = (((1,), (1,)), ((), ()))
tn_dims = (((0,), (0,)), ((), ()))


def one_hot(slots):
    experts, tokens = slots.shape
    place = lax.broadcasted_iota(jnp.int32, (experts, CAP, tokens), 1).astype(wide) + 1.0
    return (slots[:, None, :] == place).astype(wide).reshape(experts * CAP, tokens)


def dot(left, right, dims=(((1,), (0,)), ((), ()))):
    return lax.dot_general(left, right, dims, preferred_element_type=wide)


def gate_column(pick, gates):
    spread = jnp.broadcast_to(gates[:, None, :], (gates.shape[0], CAP, gates.shape[1]))
    return jnp.sum(pick * spread.reshape(pick.shape), axis=1, keepdims=True)


def product_kernel(left_ref, right_ref, out_ref):
    out_ref[...] = dot(left_ref[...], right_ref[...], nt_dims)


def turned_product(left, right, block=256):
    rows, depth = left.shape
    columns = right.shape[0]
    return pl.pallas_call(
        product_kernel,
        grid=(columns // block,),
        in_specs=[
            pl.BlockSpec((rows, depth), lambda i: (0, 0)),
            pl.BlockSpec((block, depth), lambda i: (i, 0)),
        ],
        out_specs=pl.BlockSpec((rows, block), lambda i: (0, i)),
        out_shape=jax.ShapeDtypeStruct((rows, columns), wide),
        compiler_params=pltpu.CompilerParams(vmem_limit_bytes=40 * 1024 * 1024),
        cost_estimate=pl.CostEstimate(
            flops=50 * rows * depth * columns, bytes_accessed=columns * depth * 2, transcendentals=0
        ),
        name="turned_product",
    )(left, right)


class Streams:
    def __init__(self, sources, targets, sems, rows_v, rows_hbm, row_sem, base):
        self.step, chunk = pl.program_id(0), rows_v.shape[0]
        experts = sources[0].shape[0]
        self.groups = [range(experts // 2), range(experts // 2, experts)]
        self.weights = [
            [
                pltpu.make_async_copy(source.at[e], target(e), sems.at[i, e])
                for i, (source, target) in enumerate(zip(sources, targets, strict=True))
                for e in group
            ]
            for group in self.groups
        ]
        block = base + self.step * chunk
        self.rows = [
            pltpu.make_async_copy(
                rows_v.at[:, e * CAP : (e + 1) * CAP, :],
                rows_hbm.at[e, pl.ds(block, chunk)],
                row_sem.at[e],
            )
            for e in range(experts)
        ]

        @pl.when(self.step == 0)
        def _():
            for copies in self.weights:
                for copy in copies:
                    copy.start()

        @pl.when(self.step > 0)
        def _():
            self.wait_rows()

    def wait_rows(self):
        for copy in self.rows:
            copy.wait()

    def send_rows(self):
        for copy in self.rows:
            copy.start()

    def wait_weights(self, group):
        @pl.when(self.step == 0)
        def _():
            for copy in self.weights[group]:
                copy.wait()

    def end(self):
        @pl.when(self.step == pl.num_programs(0) - 1)
        def _():
            self.wait_rows()


def write_parts(targets, block, total):
    share = total.shape[0] // len(targets)
    for i, target in enumerate(targets):
        target[block] = total[i * share : (i + 1) * share]


def forward_kernel(base, kept, parts, _, slots_ref, router_ref, x_ref, *refs):
    weights, refs = refs[:3], refs[3:]
    refs = refs[kept:]
    y_refs, refs = refs[:parts], refs[parts:]
    gates_ref, pre_ref, inner_ref, rows_hbm = refs[:4]
    joint_w, down_w, rows_v, out_v, gate_rows, w_sems, row_sems = refs[4:]
    chunk, _, width = x_ref.shape
    experts, hidden, _ = down_w.shape
    depth = chunk * CAP
    targets = (
        lambda e: joint_w.at[e, :, :hidden],
        lambda e: joint_w.at[e, :, hidden:],
        lambda e: down_w.at[e],
    )
    streams = Streams(weights, targets, w_sems, rows_v, rows_hbm, row_sems, base)
    picks = []
    for b in range(chunk):
        tokens = x_ref[b]
        logits = dot(tokens, router_ref[...]).T
        exponent = jnp.exp(logits - jnp.max(logits, axis=0, keepdims=True))
        gates = (exponent / jnp.sum(exponent, axis=0, keepdims=True))[:experts]
        gates_ref[b] = gates
        pick = one_hot(slots_ref[b])
        gate_rows[b] = gate_column(pick, gates)
        picks.append(pick.astype(low))
        rows_v[b] = dot(picks[b], tokens).astype(low)
    streams.send_rows()
    for e in range(experts):
        at = slice(e * CAP, (e + 1) * CAP)
        for i, group in enumerate(streams.groups):
            if e == group.start:
                streams.wait_weights(i)
        pre = dot(rows_v[:, at, :].reshape(depth, width), joint_w[e])
        pre_ref[e] = pre
        gate_pre, up_pre = pre[:, :hidden], pre[:, hidden:]
        inner = (gate_pre * jax.nn.sigmoid(gate_pre) * up_pre).astype(low).astype(wide)
        scaled = (inner * gate_rows[:, at, :].reshape(depth, 1)).astype(low)
        inner_ref[e] = scaled
        out = dot(scaled, down_w[e]).astype(low)
        out_v[:, at, :] = out.reshape(chunk, CAP, width)
    for b in range(chunk):
        write_parts(y_refs, b, dot(picks[b], out_v[b], tn_dims).astype(low))
    streams.end()


def backward_kernel(base, kept, parts, _, slots_ref, gates_ref, g_ref, pre_ref, *refs):
    weights, refs = refs[:3], refs[3:]
    refs = refs[kept:]
    x_refs, refs = refs[:parts], refs[parts:]
    grads_ref, dgate_ref, dup_ref, rows_hbm = refs[:4]
    joint_w, down_w, rows_v, out_v, gate_rows, grad_rows, w_sems, row_sems = refs[4:]
    chunk, _, width = g_ref.shape
    tokens = slots_ref.shape[2]
    experts, _, hidden = down_w.shape
    depth = chunk * CAP
    targets = (
        lambda e: joint_w.at[e, :hidden],
        lambda e: joint_w.at[e, hidden:],
        lambda e: down_w.at[e],
    )
    streams = Streams(weights, targets, w_sems, rows_v, rows_hbm, row_sems, base)
    picks = []
    for b in range(chunk):
        pick = one_hot(slots_ref[b])
        gate_rows[b] = gate_column(pick, gates_ref[b])
        picks.append(pick.astype(low))
        rows_v[b] = dot(picks[b], g_ref[b]).astype(low)
    streams.send_rows()
    for e in range(experts):
        at = slice(e * CAP, (e + 1) * CAP)
        for i, group in enumerate(streams.groups):
            if e == group.start:
                streams.wait_weights(i)
        pulled = dot(rows_v[:, at, :].reshape(depth, width), down_w[e])
        gate_pre, up_pre = pre_ref[e, :, :hidden], pre_ref[e, :, hidden:]
        sigmoid = jax.nn.sigmoid(gate_pre)
        silu = gate_pre * sigmoid
        inner = (silu * up_pre).astype(low).astype(wide)
        grad_rows[:, at, :] = jnp.sum(inner * pulled, axis=1, keepdims=True).reshape(
            chunk, CAP, 1
        )
        grad_inner = pulled * gate_rows[:, at, :].reshape(depth, 1)
        dgate = (grad_inner * up_pre * sigmoid * (1.0 + gate_pre * (1.0 - sigmoid))).astype(low)
        dup = (grad_inner * silu).astype(low)
        dgate_ref[e] = dgate
        dup_ref[e] = dup
        out = dot(jnp.concatenate([dgate, dup], axis=1), joint_w[e]).astype(low)
        out_v[:, at, :] = out.reshape(chunk, CAP, width)
    for b in range(chunk):
        write_parts(x_refs, b, dot(picks[b], out_v[b], tn_dims).astype(low))
        per_row = picks[b].astype(wide) * grad_rows[b]
        grads_ref[b] = jnp.sum(per_row.reshape(experts, CAP, tokens), axis=1)
    streams.end()


class Experts:
    def __init__(self, blocks, chunk, tokens, width, experts, hidden):
        self.chunk, self.half = chunk, blocks // 2
        self.tokens, self.width, self.experts, self.hidden = tokens, width, experts, hidden
        self.rows = blocks * CAP

    def mine(self, first, *shape):
        return pl.BlockSpec(
            (self.chunk,) + shape,
            lambda i, core: (2 * (i + first) + core[0],) + (0,) * len(shape),
        )

    def listed(self, first, *shape):
        return pl.BlockSpec(
            (self.chunk,) + shape, lambda i, core: (i + first,) + (0,) * len(shape)
        )

    def by_row(self, last, first):
        return pl.BlockSpec(
            (self.experts, self.chunk * CAP, last), lambda i, core: (0, i + first, 0)
        )

    def call(self, kernel, name, first, count, turn, parts, core, ins, in_specs, outs, given):
        any_spec = pl.BlockSpec(memory_space=pl.ANY)
        base = turn * self.half + first * self.chunk
        joint = [self.experts, self.width, self.width]
        joint[2 if kernel is forward_kernel else 1] = 2 * self.hidden
        given = [None] * (len(outs) - len(given)) + given
        goes_on = [i for i, array in enumerate(given) if array is not None]
        rows = self.experts * count * self.chunk * CAP
        results = pl.pallas_call(
            functools.partial(kernel, base, len(goes_on), parts),
            grid_spec=pltpu.PrefetchScalarGridSpec(
                num_scalar_prefetch=1,
                grid=(count,),
                in_specs=in_specs + [any_spec] * (3 + len(goes_on)),
                out_specs=[spec or any_spec for _, _, spec in outs],
                scratch_shapes=[pltpu.VMEM(tuple(joint), low), pltpu.VMEM(ins[-1].shape, low)]
                + [pltpu.VMEM((self.chunk, self.experts * CAP, self.width), low)] * 2
                + [pltpu.VMEM((self.chunk, self.experts * CAP, 1), wide)] * (1 if kernel is forward_kernel else 2)
                + [
                    pltpu.SemaphoreType.DMA((3, self.experts)),
                    pltpu.SemaphoreType.DMA((self.experts,)),
                ],
            ),
            out_shape=[jax.ShapeDtypeStruct(shape, kind) for shape, kind, _ in outs],
            input_output_aliases={1 + len(ins) + n: i for n, i in enumerate(goes_on)},
            compiler_params=pltpu.CompilerParams(
                dimension_semantics=("arbitrary",), vmem_limit_bytes=60 * 1024 * 1024
            ),
            cost_estimate=pl.CostEstimate(
                flops=10 * rows * self.width * (3 * self.hidden + 256),
                bytes_accessed=rows * self.width * 8,
                transcendentals=0,
            ),
            name=name,
        )(core, *ins, *(given[i] for i in goes_on))
        return list(results)

    def token_outs(self, first, parts):
        share = self.tokens // parts
        part = ((self.half, share, self.width), low, self.listed(first, share, self.width))
        by_token = (
            (self.half, self.experts, self.tokens),
            wide,
            self.listed(first, self.experts, self.tokens),
        )
        return [part] * parts + [by_token]

    def row_out(self, first, turn):
        first += turn * self.half // self.chunk
        return (
            (self.experts, self.rows, self.hidden),
            low,
            self.by_row(self.hidden, first),
        )

    def taken(self):
        return ((self.experts, self.rows // CAP, CAP, self.width), low, None)

    def forward(self, first, count, turn, parts, core, slots, router, tokens, weights, given):
        pre = (
            (self.experts, self.half * CAP, 2 * self.hidden),
            wide,
            self.by_row(2 * self.hidden, first),
        )
        return self.call(
            forward_kernel,
            "experts_forward",
            first,
            count,
            turn,
            parts,
            core,
            (slots, router, tokens, *weights),
            [
                self.mine(first, self.experts, self.tokens),
                pl.BlockSpec(router.shape, lambda i, core: (0, 0)),
                self.mine(first, self.tokens, self.width),
            ],
            self.token_outs(first, parts) + [pre, self.row_out(first, turn), self.taken()],
            given,
        )

    def backward(
        self, first, count, turn, parts, core, slots, gates, grads, pre, weights, given
    ):
        return self.call(
            backward_kernel,
            "experts_backward",
            first,
            count,
            turn,
            parts,
            core,
            (slots, gates, grads, pre, *weights),
            [
                self.mine(first, self.experts, self.tokens),
                self.listed(first, self.experts, self.tokens),
                self.mine(first, self.tokens, self.width),
                self.by_row(2 * self.hidden, first),
            ],
            self.token_outs(first, parts)
            + [self.row_out(first, turn), self.row_out(first, turn), self.taken()],
            given,
        )


def on_device(
    hidden_in,
    w_query,
    w_key,
    w_value,
    w_output,
    w_router,
    gain_attn,
    gain_ffn,
    gain_query,
    gain_key,
    w_gate,
    w_up,
    w_down,
    expert_ids,
    grad_out,
):
    tokens_dev, model_width = hidden_in.shape
    local_experts, _, hidden_units = w_gate.shape
    expert_count = w_router.shape[1]
    grid = Grid()
    blocks = grid.ep * grid.tp
    weight_rows = model_width // blocks
    both = ("ep", "tp")
    inv_root = 1.0 / math.sqrt(HEAD_DIM)

    def gathered(values):
        return lax.all_gather(values, both, axis=0, tiled=True)

    named = jnp.any(
        expert_ids[None, :, :] == jnp.arange(expert_count, dtype=jnp.int32)[:, None, None], axis=2
    )
    before = (jnp.arange(tokens_dev)[:, None] <= jnp.arange(tokens_dev)[None, :]).astype(low)
    counted = jnp.dot(named.astype(low), before, preferred_element_type=wide)
    slots = jnp.where(named, counted, 0.0).astype(low)

    shared = jnp.concatenate(
        [
            w_router,
            jnp.stack([gain_attn, gain_ffn, gain_query, gain_key], axis=1),
            jnp.zeros((w_router.shape[0], tokens_dev - expert_count - 4), low),
        ],
        axis=1,
    )
    output_full = grid.gather_second(grid.gather_first(w_output))
    small_all = after(jnp.concatenate([shared, slots], axis=0), output_full)
    small_all = grid.gather(small_all, "xyuwc")
    small_all = small_all.reshape(blocks, weight_rows + expert_count, tokens_dev)
    shared_full = small_all[:, :weight_rows].reshape(model_width, tokens_dev)
    slots_all = small_all[:, weight_rows:]
    router_full = shared_full[:, :expert_count]
    gains = shared_full[:, expert_count : expert_count + 4].astype(wide).T
    attn_gain, ffn_gain, query_gain, key_gain = gains[0], gains[1], gains[2], gains[3]

    projections = gathered(jnp.concatenate([w_query, w_key, w_value], axis=1))
    inputs_full = hidden_in.astype(wide)
    scale_attn = lax.rsqrt(jnp.mean(inputs_full * inputs_full, axis=-1, keepdims=True) + epsilon)
    unit_attn = inputs_full * scale_attn
    normed_attn = (unit_attn * attn_gain).astype(low)
    projections, output_full, normed_attn, query_gain, key_gain, ffn_gain = together(
        projections,
        output_full,
        normed_attn,
        query_gain,
        key_gain,
        ffn_gain,
    )
    upstream_all = gathered(after(grad_out, projections)[None])
    projected = jnp.dot(normed_attn, projections, preferred_element_type=wide)
    query_raw = projected[:, :model_width]
    key_raw = projected[:, model_width : 2 * model_width]
    value_raw = projected[:, 2 * model_width :]
    scale_query = lax.rsqrt(jnp.mean(query_raw * query_raw, axis=-1, keepdims=True) + epsilon)
    unit_query = query_raw * scale_query
    scale_key = lax.rsqrt(jnp.mean(key_raw * key_raw, axis=-1, keepdims=True) + epsilon)
    unit_key = key_raw * scale_key
    cosines, sines = rope_tables(tokens_dev, HEAD_DIM)
    query_rot = rotate(
        (unit_query * query_gain).reshape(tokens_dev, HEADS, HEAD_DIM), cosines, sines
    ).astype(low)
    key_rot = rotate(
        (unit_key * key_gain).reshape(tokens_dev, HEADS, HEAD_DIM), cosines, sines
    ).astype(low)
    value_heads = value_raw.astype(low).reshape(tokens_dev, HEADS, HEAD_DIM)
    causal = jnp.arange(tokens_dev)[:, None] >= jnp.arange(tokens_dev)[None, :]
    scores = (
        jnp.einsum("qhd,khd->hqk", query_rot, key_rot, preferred_element_type=wide) * inv_root
    )
    scores = jnp.where(causal[None], scores, masked_value)
    exponent = jnp.exp(scores - jnp.max(scores, axis=-1, keepdims=True))
    att_probs = exponent / jnp.sum(exponent, axis=-1, keepdims=True)
    probs_low = att_probs.astype(low)
    attended = (
        jnp.einsum("hqk,khd->qhd", probs_low, value_heads, preferred_element_type=wide)
        .reshape(tokens_dev, model_width)
        .astype(low)
    )
    mixed = inputs_full + jnp.dot(attended, output_full, preferred_element_type=wide)
    scale_ffn = lax.rsqrt(jnp.mean(mixed * mixed, axis=-1, keepdims=True) + epsilon)
    unit_ffn = mixed * scale_ffn
    normed_ffn = (unit_ffn * ffn_gain).astype(low)
    normed_all = gathered(normed_ffn[None])
    router_probs = jax.nn.softmax(
        jnp.dot(normed_ffn, router_full, preferred_element_type=wide), axis=-1
    )

    turned = [weights.transpose(0, 2, 1) for weights in (w_gate, w_up, w_down)]
    normed_all, turned = together(normed_all, turned)

    first_expert = lax.axis_index("ep") * local_experts
    slots_here = lax.dynamic_slice_in_dim(slots_all, first_expert, local_experts, 1).astype(wide)
    router_turned = lax.dynamic_slice_in_dim(
        jnp.concatenate([router_full, router_full], axis=1), first_expert, expert_count, 1
    )
    experts = Experts(
        blocks, grid.tp, tokens_dev, model_width, local_experts, hidden_units
    )
    core = grid.place("c")
    turns = (jnp.reshape(1 - core, (1,)), jnp.reshape(core, (1,)))
    chips = grid.chips()

    def token_sums(away, kept):
        return [
            [half.reshape(chips + half.shape[1:]) for half in pair]
            for pair in zip(away, kept, strict=True)
        ]

    groups = blocks // 2 // grid.tp
    forward_ins = (slots_here, router_turned, normed_all, (w_gate, w_up, w_down))
    *y_ahead, gates_ahead, pre_ahead, inner_scaled, rows_in = experts.forward(
        0, groups, 0, 2, turns[0], *forward_ins, []
    )
    *y_own, gates_own, pre_own, inner_scaled, rows_in = experts.forward(
        0, groups, 1, 2, turns[1], *forward_ins, [inner_scaled, rows_in]
    )
    y_away = [grid.shift(half, "c", 1) for half in y_ahead]
    y_own, y_away, gates_own, slots_here = together(y_own, y_away, gates_own, slots_here)
    expert_sums = token_sums(y_away, y_own)
    cuts = grid.first_cuts(expert_sums)
    cuts, upstream_all, slots_here = together(cuts, upstream_all, slots_here)

    def backward(first, count, turn, parts, gates, pre, given):
        return experts.backward(
            first,
            count,
            turn,
            parts,
            turns[turn],
            slots_here,
            gates,
            upstream_all,
            pre,
            turned,
            given,
        )

    def by_core(values):
        parts = jnp.split(values, 2 * chips[0] * chips[1], axis=1)
        cut = [jnp.concatenate(parts[at::2], axis=1) for at in range(2)]
        return [chosen(at, cut) for at in (1 - core, core)]

    away, kept = (
        jnp.concatenate(cut, axis=1)
        for cut in zip(by_core(normed_attn), by_core(attended), strict=True)
    )
    ahead = backward(0, groups, 0, 2, gates_ahead, pre_ahead, [])
    expert_sums = grid.reduce_first(expert_sums, cuts)
    pair_rows = [kept, grid.shift(away, "c", 1)]
    (*x_ahead, gate_grads_ahead, dgate, dup, taken), expert_sums, slots_here, pair_rows = together(
        ahead, expert_sums, slots_here, pair_rows
    )
    x_away = [grid.shift(half, "c", 1) for half in x_ahead]
    own = backward(0, groups, 1, 2, gates_own, pre_own, [dgate, dup, taken])
    expert_sum = grid.reduce_second(expert_sums, 0)
    own, expert_sum, x_away = together(own, expert_sum, x_away)
    *x_own, gate_grads_own, grad_gate_part, grad_up_part, rows_up = own
    rows_in = rows_in.reshape(local_experts, -1, model_width)
    rows_up = rows_up.reshape(local_experts, -1, model_width)

    def weight_grad(subscripts, left, right):
        return jnp.einsum(subscripts, left, right, preferred_element_type=wide)

    sums = token_sums(x_away, x_own)
    gate_grads = jnp.stack([gate_grads_own, gate_grads_ahead])
    gate_grads = jnp.where(core == 0, gate_grads, gate_grads[::-1])
    gate_grads = gate_grads.reshape((2,) + chips + (local_experts, tokens_dev))
    acc_gate = weight_grad("erd,erh->edh", rows_in, grad_gate_part)
    acc_down = weight_grad("erh,erd->ehd", inner_scaled, rows_up)
    sums = grid.reduce_first(sums)
    expert_sum = grid.reduce_axis(expert_sum, "w", "uw")
    gate_grads = grid.reduce_axis(gate_grads, "w", "cyxuw")
    sums, acc_gate, acc_down, expert_sum, rows_in, gate_grads = together(
        sums, acc_gate, acc_down, expert_sum, rows_in, gate_grads
    )
    acc_up = weight_grad("erd,erh->edh", rows_in, grad_up_part)
    sums = grid.reduce_second(sums, None)
    expert_sum = grid.reduce_axis(expert_sum, "u", "u")
    gate_grads = grid.reduce_axis(gate_grads, "u", "cyxu")
    gate_grads = lax.dynamic_update_slice_in_dim(
        jnp.zeros(gate_grads.shape[:3] + (expert_count, tokens_dev), wide),
        gate_grads,
        first_expert,
        3,
    )
    sums, acc_up, expert_sum, gate_grads, pair_rows = together(
        sums, acc_up, expert_sum, gate_grads, pair_rows
    )
    block_out = (mixed + expert_sum.astype(wide)).astype(low)
    sums = grid.reduce_z(sums, 0)
    gate_grads = grid.reduce_axis(gate_grads, "c", "cyx")
    pair_rows = jnp.concatenate(pair_rows, axis=0)
    half = model_width // 2
    y_rows = grid.from_line(pair_rows[:, :half], "y")
    x_rows = grid.from_line(pair_rows, "x")
    sums, gate_grads, y_rows, x_rows = together(sums, gate_grads, y_rows, x_rows)
    back_sum = jnp.concatenate(grid.reduce_z(sums, 1), axis=0)
    grad_probs = grid.reduce_scatter(gate_grads, "yx", "yx").T
    y_rows, x_rows = jnp.concatenate(y_rows, axis=0), jnp.concatenate(x_rows, axis=0)
    back_sum, grad_probs, y_rows, x_rows = together(back_sum, grad_probs, y_rows, x_rows)
    back_sum, block_out, acc_gate, acc_up, acc_down = together(
        back_sum, block_out, acc_gate, acc_up, acc_down
    )

    upstream = grad_out.astype(wide)
    grad_logits = router_probs * (
        grad_probs - jnp.sum(router_probs * grad_probs, axis=-1, keepdims=True)
    )
    grad_ffn_normed = back_sum.astype(wide) + jnp.dot(
        grad_logits, router_full.astype(wide).T, precision=lax.Precision.HIGHEST
    )
    grad_ffn_gain = jnp.sum(grad_ffn_normed * unit_ffn, axis=0)
    grad_mixed = upstream + rms_back(grad_ffn_normed, unit_ffn, ffn_gain, scale_ffn)
    grad_branch = grad_mixed.astype(low)

    output_columns = grid.columns_from_line(grad_branch, "x")
    grad_attended = jnp.einsum(
        "te,de->td", grad_branch, output_full, preferred_element_type=wide
    ).astype(low)
    grad_heads = grad_attended.reshape(tokens_dev, HEADS, HEAD_DIM)
    grad_value_rows = (
        jnp.einsum("hqk,qhd->khd", probs_low, grad_heads, preferred_element_type=wide)
        .reshape(tokens_dev, model_width)
        .astype(low)
    )
    value_columns = grid.columns_from_line(grad_value_rows, "y")
    grad_probs_att = jnp.einsum(
        "qhd,khd->hqk", grad_heads, value_heads, preferred_element_type=wide
    )
    grad_scores = (
        att_probs * (grad_probs_att - jnp.sum(att_probs * grad_probs_att, axis=-1, keepdims=True))
    ).astype(low)
    grad_qrot = (
        jnp.einsum("hqk,khd->qhd", grad_scores, key_rot, preferred_element_type=wide) * inv_root
    )
    grad_krot = (
        jnp.einsum("hqk,qhd->khd", grad_scores, query_rot, preferred_element_type=wide) * inv_root
    )
    grad_qnorm = unrotate(bounce(grad_qrot), cosines, sines).reshape(tokens_dev, model_width)
    grad_knorm = unrotate(bounce(grad_krot), cosines, sines).reshape(tokens_dev, model_width)
    grad_query_gain = jnp.sum(grad_qnorm * unit_query, axis=0)
    grad_key_gain = jnp.sum(grad_knorm * unit_key, axis=0)
    grad_query_raw = rms_back(grad_qnorm, unit_query, query_gain, scale_query).astype(low)
    grad_key_raw = rms_back(grad_knorm, unit_key, key_gain, scale_key).astype(low)
    output_columns, value_columns, grad_query_raw, grad_key_raw = together(
        output_columns, value_columns, grad_query_raw, grad_key_raw
    )

    def outer(left, right):
        total = jnp.einsum("tc,te->ce", left, right, preferred_element_type=wide)
        return total.astype(low).reshape(chips + (weight_rows, -1))

    first = [
        outer(x_rows[:, half:], output_columns),
        outer(y_rows, value_columns),
    ]
    second = [
        grid.columns_from_line(grad_query_raw, "x"),
        grid.columns_from_line(grad_key_raw, "y"),
    ]
    grads = jnp.concatenate([grad_query_raw, grad_key_raw, grad_value_rows], axis=1)
    first, second, grads = together(first, second, grads)
    first = grid.reduce_first(first)
    second = [
        outer(x_rows[:, :half], second[0]),
        outer(y_rows, second[1]),
    ]
    grad_attn_normed = turned_product(grads, projections)
    first, second, grad_attn_normed, grad_logits = together(
        first, second, grad_attn_normed, grad_logits
    )
    grad_router_local = jnp.dot(
        normed_ffn.astype(wide).T, grad_logits, precision=lax.Precision.HIGHEST
    )
    grad_attn_gain = jnp.sum(grad_attn_normed * unit_attn, axis=0)
    grad_input = grad_mixed + rms_back(grad_attn_normed, unit_attn, attn_gain, scale_attn)
    gain_sums = jnp.stack(
        [grad_attn_gain, grad_ffn_gain, grad_query_gain, grad_key_gain], axis=1
    )
    small_sums = jnp.concatenate([grad_router_local, gain_sums], axis=1).reshape(
        grid.shape + (weight_rows, expert_count + gain_sums.shape[1])
    )
    first = grid.reduce_z(first, 0, "xy")
    second = grid.reduce_first(second)
    first, second, small_sums = together(first, second, small_sums)
    first = grid.reduce_z(first, 1, "xy")
    second = grid.reduce_z(second, 0, "xy")
    small_sums = grid.reduce_scatter(small_sums, "cy")
    first, second, small_sums = together(first, second, small_sums)
    grad_output, grad_value = grid.rows_of_both(first)
    second = grid.reduce_z(second, 1, "xy")
    small_sums = grid.reduce_scatter(small_sums, "x", "xuw")
    grad_output, grad_value, second, small_sums = together(
        grad_output, grad_value, second, small_sums
    )
    grad_query, grad_key = grid.rows_of_both(second)
    small_sums = small_sums.reshape((-1,) + small_sums.shape[2:])
    small_sums = grid.reduce_axis(small_sums, "z", "z")
    return (
        block_out,
        grad_input,
        grad_query,
        grad_key,
        grad_value,
        grad_output,
        small_sums[:, :expert_count],
        *(small_sums[:, expert_count + i] for i in range(4)),
        acc_gate,
        acc_up,
        acc_down,
    )


def solution(mesh):
    placed = (
        P(("ep", "tp"), None),
        P(("ep", "tp"), None),
        P(("ep", "tp"), None),
        P(("ep", "tp"), None),
        P(("ep", "tp"), None),
        P(("ep", "tp"), None),
        P(("ep", "tp")),
        P(("ep", "tp")),
        P(("ep", "tp")),
        P(("ep", "tp")),
        P("ep", None, "tp"),
        P("ep", None, "tp"),
        P("ep", "tp", None),
        P(("ep", "tp"), None),
        P(("ep", "tp"), None),
    )
    return jax.shard_map(
        on_device,
        mesh=mesh,
        in_specs=placed,
        out_specs=(
            P(("ep", "tp"), None),
            P(("ep", "tp"), None),
            P(("ep", "tp"), None),
            P(("ep", "tp"), None),
            P(("ep", "tp"), None),
            P(("ep", "tp"), None),
            P(("ep", "tp"), None),
            P(("ep", "tp")),
            P(("ep", "tp")),
            P(("ep", "tp")),
            P(("ep", "tp")),
            P("ep", None, "tp"),
            P("ep", None, "tp"),
            P("ep", "tp", None),
        ),
        check_vma=False,
    )
```
